32 devices in a mesh: groups: 2 (over y), seq: 8 (over z, x), heads: 2 (over core).
Axes of the slice: x: 2, y: 2, z: 4, core: 2. Of those that a mesh axis runs over, the one named last changes fastest.
Arguments:
- queries: bfloat16 [4096, 16, 128], P(('groups', 'seq'), 'heads'), parts along dimension 0, may hold values from -20 to 20
- keys: bfloat16 [4096, 16, 128], P(('groups', 'seq'), 'heads'), parts along dimension 0, may hold values from -18 to 18
- values: bfloat16 [4096, 16, 128], P(('groups', 'seq'), 'heads'), parts along dimension 0, may hold values from -6 to 6
- out_grad: bfloat16 [4096, 16, 128], P(('groups', 'seq'), 'heads'), parts along dimension 0, may hold values from -6 to 6
- spans: int32 [3, 4096], P(None, ('groups', 'seq')), parts along dimension 1, may hold values from 0 to 2048, as said below
Outputs:
- attended: bfloat16 [4096, 16, 128], P(('groups', 'seq'), 'heads'), parts along dimension 0
- query_grad: bfloat16 [4096, 16, 128], P(('groups', 'seq'), 'heads'), parts along dimension 0
- key_grad: bfloat16 [4096, 16, 128], P(('groups', 'seq'), 'heads'), parts along dimension 0
- value_grad: bfloat16 [4096, 16, 128], P(('groups', 'seq'), 'heads'), parts along dimension 0
The draws below stay inside these ranges and needn't reach their ends.
There are 2 independent parts, one for each index of `groups`. The reference program is written for one: setup_inputs(seed, part) draws one part's arguments, and reference() takes and returns one part's arrays. A program takes and returns all parts, laid end to end along the dimension named above; each array names one. Nothing has to cross between parts.
Inputs may be any that keep to these rules, and one draw needn't show every extreme that they name: Triples lie end to end from position 0; for each token spans[0] <= position, spans[0] < spans[1] <= spans[2], and all tokens of a triple share the three values. A triple holds at most 512 tokens, and one holds exactly 512. The triple that holds the last token has spans[2] = 2048.
All inputs are finite; a program needn't handle non-finite values.
Results may differ from the reference program's by a relative error of at most 0.022.
Values may be sent and summed in bfloat16 or wider, within the bound.
A program may use at most 64 MiB of HBM per device.

```python
import math
import jax
import jax.numpy as jnp
from jax import lax

HEADS = 16
HD = 128
REACH = 2
TOK_DEV = 256
SEQ = 2048
TRIPLE_MAX = 512


def joint_fields(key):
    base = jax.random.fold_in(key, 101)
    seed_query, seed_keys = jax.random.split(base, 2)
    field_shape = (SEQ, HEADS, HD)
    query_field = jnp.clip(jax.random.normal(seed_query, field_shape, jnp.float32), -6.0, 6.0)
    key_field = jnp.clip(jax.random.normal(seed_keys, field_shape, jnp.float32), -6.0, 6.0)
    return (query_field, key_field)


def draw_queries(key, part):
    return joint_fields(key)[0].astype(jnp.bfloat16)


def draw_keys(key, part):
    return joint_fields(key)[1].astype(jnp.bfloat16)


def draw_spans(key, part):
    base = jax.random.fold_in(key, 202)
    seed_length, seed_prompt, seed_chosen, seed_longest = jax.random.split(base, 4)
    shortest = TRIPLE_MAX // 4
    triple_count = SEQ // shortest + 2
    lengths = jax.random.randint(seed_length, (triple_count,), shortest, TRIPLE_MAX + 1)
    longest = jax.random.randint(seed_longest, (), 0, max(SEQ // TRIPLE_MAX, 1))
    triple_index = jnp.arange(triple_count)
    lengths = jnp.where(triple_index == longest, TRIPLE_MAX, lengths)
    triple_ends = jnp.cumsum(lengths)
    triple_starts = triple_ends - lengths
    prompt = 1 + (lengths - 3) * jax.random.randint(seed_prompt, (triple_count,), 20, 51) // 100
    chosen = 1 + (lengths - 2 - prompt) * jax.random.randint(seed_chosen, (triple_count,), 30, 71) // 100
    positions = jnp.arange(SEQ)
    owner = jnp.sum((triple_ends[None, :] <= positions[:, None]).astype(jnp.int32), axis=1)
    final_owner = owner[SEQ - 1]
    triple_first = triple_starts[owner]
    chosen_first = jnp.minimum(triple_first + prompt[owner], SEQ)
    rejected_first = jnp.where(owner == final_owner, SEQ, jnp.minimum(chosen_first + chosen[owner], SEQ))
    return jnp.stack((triple_first, chosen_first, rejected_first)).astype(jnp.int32)


def steps_of(own_key, extent, cuts, low, high):
    def one(axis_at, blocks):
        steps = jax.random.uniform(jax.random.fold_in(jax.random.fold_in(own_key, 6), axis_at), (blocks,), jnp.float32, low / len(cuts), high / len(cuts))
        return jnp.repeat(jnp.exp(steps), extent[axis_at] // blocks).reshape((-1,) + (1,) * (len(extent) - axis_at - 1))

    factor_of = one(*cuts[0])
    for cut in cuts[1:]:
        factor_of = factor_of * one(*cut)
    return factor_of


def gaussian(key, dims, spread, reach, pieces=(), kind=jnp.bfloat16):
    loudness = steps_of(key, dims, pieces, -0.22, 0.18) if pieces else 1.0
    values = jax.random.normal(key, dims, jnp.float32) * spread * loudness
    return jnp.minimum(jnp.maximum(values, -reach), reach).astype(kind)


def setup_inputs(seed: int = 0, part: int = 0) -> dict:
    splits = jax.random.split(jax.random.key(seed), 6)
    own_keys = jax.random.split(jax.random.fold_in(splits[5], part), 6)
    return {
        "queries": draw_queries(jax.random.fold_in(jax.random.fold_in(splits[5], part), 71), part),
        "keys": draw_keys(jax.random.fold_in(jax.random.fold_in(splits[5], part), 71), part),
        "values": gaussian(own_keys[2], (SEQ, HEADS, HD), 1.0, 6.0, ((0, 8), (1, 2))),
        "out_grad": gaussian(own_keys[3], (SEQ, HEADS, HD), 1.0, 6.0, ((0, 8), (1, 2))),
        "spans": draw_spans(jax.random.fold_in(jax.random.fold_in(splits[5], part), 71), part),
    }


NEG = -1e+30

def rounded(tensor):
    return lax.optimization_barrier(tensor.astype(jnp.bfloat16)).astype(jnp.float32)

def reference(queries, keys, values, out_grad, spans):
    score_scale = 1.0 / math.sqrt(HD)
    reach_rows = REACH * TOK_DEV
    window = reach_rows + TOK_DEV
    padding = ((reach_rows, 0), (0, 0), (0, 0))
    keys_padded = jnp.pad(keys, padding)
    values_padded = jnp.pad(values, padding)
    offsets = jnp.arange(TOK_DEV, dtype=jnp.int32)
    window_offsets = jnp.arange(window, dtype=jnp.int32)
    block_count = SEQ // TOK_DEV

    def step_block(accumulated, block_index):
        anchor = (block_index * TOK_DEV).astype(jnp.int32)
        query_pos = anchor + offsets
        key_pos = anchor - reach_rows + window_offsets
        starts = lax.dynamic_slice_in_dim(spans[0], anchor, TOK_DEV)
        chosen = lax.dynamic_slice_in_dim(spans[1], anchor, TOK_DEV)
        rejected = lax.dynamic_slice_in_dim(spans[2], anchor, TOK_DEV)
        allowed = (key_pos[None, :] >= starts[:, None]) & (key_pos[None, :] <= query_pos[:, None])
        crossed = (query_pos >= rejected)[:, None] & (key_pos[None, :] >= chosen[:, None]) & (key_pos[None, :] < rejected[:, None])
        visible = allowed & jnp.logical_not(crossed)
        query_block = lax.dynamic_slice_in_dim(queries, anchor, TOK_DEV).astype(jnp.float32)
        grad_block = lax.dynamic_slice_in_dim(out_grad, anchor, TOK_DEV).astype(jnp.float32)
        key_block = lax.dynamic_slice_in_dim(keys_padded, anchor, window).astype(jnp.float32)
        value_block = lax.dynamic_slice_in_dim(values_padded, anchor, window).astype(jnp.float32)
        scores = jnp.einsum('qhd,khd->hqk', query_block, key_block) * score_scale
        scores = jnp.where(visible[None], scores, NEG)
        row_max = lax.optimization_barrier(jnp.max(scores, axis=-1))
        weights = jnp.exp(scores - row_max[..., None])
        row_sum = lax.optimization_barrier(jnp.sum(weights, axis=-1))
        mixed = jnp.einsum('hqk,khd->qhd', rounded(weights), value_block)
        attended = (mixed / row_sum.T[:, :, None]).astype(jnp.bfloat16)
        log_total = row_max + jnp.log(row_sum)
        probs = jnp.exp(scores - log_total[..., None])
        delta = lax.optimization_barrier(jnp.sum(grad_block * attended.astype(jnp.float32), axis=-1)).T
        value_part = jnp.einsum('hqk,qhd->khd', rounded(probs), grad_block)
        prob_grad = jnp.einsum('qhd,khd->hqk', grad_block, value_block)
        score_grad = rounded(probs * (prob_grad - delta[..., None]))
        query_grad = (jnp.einsum('hqk,khd->qhd', score_grad, key_block) * score_scale).astype(jnp.bfloat16)
        key_part = jnp.einsum('hqk,qhd->khd', score_grad, query_block) * score_scale
        current = lax.dynamic_slice_in_dim(accumulated, anchor, window, axis=1)
        updated = current + jnp.stack((key_part, value_part))
        accumulated = lax.dynamic_update_slice_in_dim(accumulated, updated, anchor, axis=1)
        return (accumulated, (attended, query_grad))
    initial = jnp.zeros((2, SEQ + reach_rows, HEADS, HD), jnp.float32)
    accumulated, (attended, query_grad) = lax.scan(step_block, initial, jnp.arange(block_count, dtype=jnp.int32))
    attended = attended.reshape(SEQ, HEADS, HD)
    query_grad = query_grad.reshape(SEQ, HEADS, HD)
    key_grad = accumulated[0, reach_rows:].astype(jnp.bfloat16)
    value_grad = accumulated[1, reach_rows:].astype(jnp.bfloat16)
    return (attended, query_grad, key_grad, value_grad)
```

```python
import functools
import math

import jax
import jax.numpy as jnp
from jax import lax
from jax.experimental import pallas as pl
from jax.experimental.pallas import tpu as pltpu
from jax.sharding import PartitionSpec as P

NEG = -1e30
MESH = pl.DeviceIdType.MESH
F32 = jnp.float32
BF16 = jnp.bfloat16


def dot_nt(a, b):
    return lax.dot_general(a, b, (((1,), (1,)), ((), ())), preferred_element_type=F32)


def dot_tn(a, b):
    return lax.dot_general(a, b, (((0,), (0,)), ((), ())), preferred_element_type=F32)


def dot_nn(a, b):
    return lax.dot_general(a, b, (((1,), (0,)), ((), ())), preferred_element_type=F32)


def kernel(
    count, tok, half, head_size,
    arg_ref, spans_ref, out_ref,
    kv, qd, span_own, span_other, bias, s_buf, dp_buf, grads, halo_out, halo_back, od, last,
    span_sem, kv_sem, qd_sem, own_sem, fwd_sem, back_sem, od_sem, last_sem,
):
    me = lax.axis_index("seq")
    x = lax.rem(me, 2)
    other = 1 - x
    pair = lax.div(me, 2)
    partner = me + 1 - 2 * x
    has_next = me + 2 < count
    has_prev = me >= 2
    score_scale = 1.0 / math.sqrt(head_size)

    def remote(src, dst, sems, at, to):
        return pltpu.make_async_remote_copy(
            src_ref=src,
            dst_ref=dst,
            send_sem=sems.at[(0,) + at],
            recv_sem=sems.at[(1,) + at],
            device_id={"seq": to},
            device_id_type=MESH,
        )

    def send_spans():
        return remote(span_own, span_other, span_sem, (), partner)

    def send_kv(i):
        src = arg_ref.at[other * half + i, pl.ds(0, 2)]
        return remote(src, kv.at[i, :, 2 + x], kv_sem, (i,), partner)

    def send_qd(i):
        src = arg_ref.at[other * half + i, pl.ds(2, 2)]
        return remote(src, qd.at[i, x], qd_sem, (i,), partner)

    def send_own(i):
        src = arg_ref.at[x * half + i, pl.ds(0, 2)]
        return remote(src, kv.at[i, :, x], own_sem, (i,), me + 2)

    def send_fwd(i):
        return remote(kv.at[i, :, 2 + other], kv.at[i, :, other], fwd_sem, (i,), me + 2)

    def send_back(i, block):
        return remote(halo_out.at[i, block], halo_back.at[i, block], back_sem, (i, block), me - 2)

    def send_od(i):
        dst = out_ref.at[x * half + i, pl.ds(0, 2)]
        return remote(od.at[i, other], dst, od_sem, (i,), partner)

    def send_last(i):
        dst = out_ref.at[x * half + i, pl.ds(2, 2)]
        return remote(last.at[i], dst, last_sem, (i,), partner)

    def land_kv(i):
        dst = kv.at[i, :, 2 + other]
        return remote(arg_ref.at[0, pl.ds(0, 2)], dst, kv_sem, (i,), partner)

    def land_qd(i):
        return remote(arg_ref.at[0, pl.ds(2, 2)], qd.at[i, other], qd_sem, (i,), partner)

    def land_own(i):
        return remote(arg_ref.at[0, pl.ds(0, 2)], kv.at[i, :, x], own_sem, (i,), partner)

    def land_fwd(i):
        return remote(arg_ref.at[0, pl.ds(0, 2)], kv.at[i, :, other], fwd_sem, (i,), partner)

    def land_back(i, block):
        return send_back(i, block)

    def land_od(i):
        dst = out_ref.at[other * half + i, pl.ds(0, 2)]
        return remote(last.at[i], dst, od_sem, (i,), partner)

    def land_last(i):
        dst = out_ref.at[other * half + i, pl.ds(2, 2)]
        return remote(last.at[i], dst, last_sem, (i,), partner)

    barrier = pltpu.get_barrier_semaphore()
    pl.semaphore_signal(barrier, inc=1, device_id={"seq": partner}, device_id_type=MESH)

    @pl.when(has_next)
    def _():
        pl.semaphore_signal(barrier, inc=1, device_id={"seq": me + 2}, device_id_type=MESH)

    @pl.when(has_prev)
    def _():
        pl.semaphore_signal(barrier, inc=1, device_id={"seq": me - 2}, device_id_type=MESH)

    span_own[...] = jnp.zeros_like(span_own)
    span_own[0:3, :] = spans_ref[...]
    pl.semaphore_wait(barrier, 1 + has_next.astype(jnp.int32) + has_prev.astype(jnp.int32))

    send_spans().start()
    for i in range(half):
        send_kv(i).start()
        send_qd(i).start()

    @pl.when(has_next)
    def _():
        for i in range(half):
            send_own(i).start()

    @pl.when(jnp.logical_not(has_prev))
    def _():
        for i in range(half):
            for which in range(2):
                kv[i, which, 0:2] = jnp.zeros((2, tok, head_size), BF16)

    @pl.when(jnp.logical_not(has_next))
    def _():
        halo_back[...] = jnp.zeros_like(halo_back)

    for i in range(half):
        kv[i, :, 2 + x] = arg_ref[x * half + i, 0:2]
        qd[i, x] = arg_ref[x * half + i, 2:4]

    send_spans().wait_recv()
    lane = lax.broadcasted_iota(jnp.int32, (1, tok), 1)
    for block in range(2):
        mine = x == block
        start_at = pair * (2 * tok) + block * tok
        low, chosen, rejected = [
            jnp.where(mine, span_own[r : r + 1, :], span_other[r : r + 1, :]) - start_at
            for r in range(3)
        ]
        chosen = jnp.where(lane >= rejected, chosen, 2 * tok)
        for part in range(3):
            at = lax.broadcasted_iota(jnp.int32, (tok, tok), 0) + (part - 2) * tok
            seen = (at >= low) & (at <= lane) & ((at < chosen) | (at >= rejected))
            bias[block, part] = jnp.where(seen, 0.0, NEG)

    def compute(i):
        for block in range(2):
            queries = qd[i, block, 0]
            out_grad = qd[i, block, 1]
            row_max = jnp.full((1, tok), -jnp.inf, F32)
            for part in range(3):
                raw = dot_nt(kv[i, 0, block + part], queries)
                scores = raw * (score_scale * math.log2(math.e)) + bias[block, part]
                s_buf[part] = scores
                row_max = jnp.maximum(row_max, jnp.max(scores, axis=0, keepdims=True))
            row_sum = jnp.zeros((1, tok), F32)
            delta = jnp.zeros((1, tok), F32)
            mixed = jnp.zeros((head_size, tok), F32)
            for part in range(3):
                weights = jnp.exp2(s_buf[part] - row_max)
                row_sum = row_sum + jnp.sum(weights, axis=0, keepdims=True)
                values = kv[i, 1, block + part]
                prob_grad = dot_nt(values, out_grad)
                delta = delta + jnp.sum(weights * prob_grad, axis=0, keepdims=True)
                s_buf[part] = weights
                dp_buf[part] = prob_grad
                mixed = mixed + dot_tn(values, weights.astype(BF16))
            inverse = 1.0 / row_sum
            delta = delta * inverse
            od[i, block, 0] = (mixed * inverse).T.astype(BF16)
            query_grad = jnp.zeros((head_size, tok), F32)
            for part in range(3):
                probs = s_buf[part] * inverse
                score_grad = (probs * (dp_buf[part] - delta)).astype(BF16)
                value_part = dot_nn(probs.astype(BF16), out_grad)
                key_part = dot_nn(score_grad, queries) * score_scale
                query_grad = query_grad + dot_tn(kv[i, 0, block + part], score_grad)
                at = block + part
                if block == 1 and part < 2:
                    key_part = key_part + grads[i, at, 0]
                    value_part = value_part + grads[i, at, 1]
                grads[i, at, 0] = key_part
                grads[i, at, 1] = value_part
            od[i, block, 1] = (query_grad * score_scale).T.astype(BF16)

    def finish(i):
        @pl.when(has_next)
        def _():
            land_back(i, other).wait_recv()

        last[i] = (grads[i, 2 + other] + halo_back[i, other].astype(F32)).astype(BF16)
        send_last(i).start()

        @pl.when(has_next)
        def _():
            land_back(i, x).wait_recv()

        done = grads[i, 2 + x] + halo_back[i, x].astype(F32)
        out_ref[x * half + i, 2:4] = done.astype(BF16)

    def step(i, carry):
        land_kv(i).wait_recv()

        @pl.when(has_next)
        def _():
            send_fwd(i).start()

        land_qd(i).wait_recv()

        @pl.when(has_prev)
        def _():
            land_own(i).wait_recv()
            land_fwd(i).wait_recv()

        compute(i)

        @pl.when(has_prev)
        def _():
            halo_out[i] = grads[i, 0:2].astype(BF16)
            send_back(i, other).start()
            send_back(i, x).start()

        send_od(i).start()
        out_ref[x * half + i, 0:2] = od[i, x]

        @pl.when(i > 0)
        def _():
            finish(i - 1)

        return carry

    lax.fori_loop(0, half, step, 0)
    finish(half - 1)

    send_spans().wait_send()
    for i in range(half):
        send_kv(i).wait_send()
        send_qd(i).wait_send()
        send_od(i).wait_send()
        send_last(i).wait_send()
        land_od(i).wait_recv()
        land_last(i).wait_recv()

    @pl.when(has_next)
    def _():
        for i in range(half):
            send_own(i).wait_send()
            send_fwd(i).wait_send()

    @pl.when(has_prev)
    def _():
        for i in range(half):
            send_back(i, other).wait_send()
            send_back(i, x).wait_send()


def per_device(count, queries, keys, values, out_grad, spans):
    tok, heads, head_size = queries.shape
    half = heads // 2
    packed = jnp.stack([a.transpose(1, 0, 2) for a in (keys, values, queries, out_grad)], axis=1)
    vmem = pltpu.VMEM
    dma = pltpu.SemaphoreType.DMA
    blocks = 3 * 2 * heads // 2
    out = pl.pallas_call(
        functools.partial(kernel, count, tok, half, head_size),
        out_shape=jax.ShapeDtypeStruct((heads, 4, tok, head_size), BF16),
        in_specs=[pl.BlockSpec(memory_space=vmem)] * 2,
        out_specs=pl.BlockSpec(memory_space=vmem),
        scratch_shapes=[
            vmem((half, 2, 4, tok, head_size), BF16),
            vmem((half, 2, 2, tok, head_size), BF16),
            vmem((8, tok), jnp.int32),
            vmem((8, tok), jnp.int32),
            vmem((2, 3, tok, tok), F32),
            vmem((3, tok, tok), F32),
            vmem((3, tok, tok), F32),
            vmem((half, 4, 2, tok, head_size), F32),
            vmem((half, 2, 2, tok, head_size), BF16),
            vmem((half, 2, 2, tok, head_size), BF16),
            vmem((half, 2, 2, tok, head_size), BF16),
            vmem((half, 2, tok, head_size), BF16),
            dma((2,)),
            dma((2, half)),
            dma((2, half)),
            dma((2, half)),
            dma((2, half)),
            dma((2, half, 2)),
            dma((2, half)),
            dma((2, half)),
        ],
        compiler_params=pltpu.CompilerParams(
            collective_id=0, has_side_effects=True, vmem_limit_bytes=48 * 1024 * 1024
        ),
        cost_estimate=pl.CostEstimate(
            flops=blocks * 12 * tok * tok * head_size,
            bytes_accessed=16 * heads * tok * head_size,
            transcendentals=blocks * tok * tok,
        ),
    )(packed, spans)
    return tuple(out[:, r].transpose(1, 0, 2) for r in range(4))


def solution(mesh):
    spec = P(("groups", "seq"), "heads", None)
    return jax.shard_map(
        functools.partial(per_device, mesh.shape["seq"]),
        mesh=mesh,
        in_specs=(spec,) * 4 + (P(None, ("groups", "seq")),),
        out_specs=(spec,) * 4,
        check_vma=False,
    )
```

```python
import functools
import math

import jax
import jax.numpy as jnp
from jax import lax
from jax.experimental import pallas as pl
from jax.experimental.pallas import tpu as pltpu
from jax.sharding import PartitionSpec as P

NEG = -1e30
MESH = pl.DeviceIdType.MESH
F32 = jnp.float32
BF16 = jnp.bfloat16


def dot_nt(a, b):
    return lax.dot_general(a, b, (((1,), (1,)), ((), ())), preferred_element_type=F32)


def dot_tn(a, b):
    return lax.dot_general(a, b, (((0,), (0,)), ((), ())), preferred_element_type=F32)


def dot_nn(a, b):
    return lax.dot_general(a, b, (((1,), (0,)), ((), ())), preferred_element_type=F32)


def kernel(
    count, tok, half, head_size,
    key_ref, value_ref, query_ref, grad_ref, spans_ref,
    att_out, query_out, key_out, value_out,
    arg_ref, stage, od_in, last_in, kv, qd, span_own, span_other, bias, s_buf, dp_buf, grads, halo_out, halo_back, od, last,
    span_sem, kv_sem, qd_sem, own_sem, fwd_sem, back_sem, od_sem, last_sem,
):
    me = lax.axis_index("seq")
    x = lax.rem(me, 2)
    other = 1 - x
    pair = lax.div(me, 2)
    partner = me + 1 - 2 * x
    has_next = me + 2 < count
    has_prev = me >= 2
    score_scale = 1.0 / math.sqrt(head_size)

    def remote(src, dst, sems, at, to):
        return pltpu.make_async_remote_copy(
            src_ref=src,
            dst_ref=dst,
            send_sem=sems.at[(0,) + at],
            recv_sem=sems.at[(1,) + at],
            device_id={"seq": to},
            device_id_type=MESH,
        )

    def send_spans():
        return remote(span_own, span_other, span_sem, (), partner)

    def send_kv(i):
        src = arg_ref.at[other * half + i, pl.ds(0, 2)]
        return remote(src, kv.at[i, :, 2 + x], kv_sem, (i,), partner)

    def send_qd(i):
        src = arg_ref.at[other * half + i, pl.ds(2, 2)]
        return remote(src, qd.at[i, x], qd_sem, (i,), partner)

    def send_own(i):
        src = arg_ref.at[x * half + i, pl.ds(0, 2)]
        return remote(src, kv.at[i, :, x], own_sem, (i,), me + 2)

    def send_fwd(i):
        return remote(kv.at[i, :, 2 + other], kv.at[i, :, other], fwd_sem, (i,), me + 2)

    def send_back(i, block):
        return remote(halo_out.at[i, block], halo_back.at[i, block], back_sem, (i, block), me - 2)

    def send_od(i):
        return remote(od.at[i, other], od_in.at[i], od_sem, (i,), partner)

    def send_last(i):
        return remote(last.at[i], last_in.at[i], last_sem, (i,), partner)

    def land_kv(i):
        dst = kv.at[i, :, 2 + other]
        return remote(arg_ref.at[0, pl.ds(0, 2)], dst, kv_sem, (i,), partner)

    def land_qd(i):
        return remote(arg_ref.at[0, pl.ds(2, 2)], qd.at[i, other], qd_sem, (i,), partner)

    def land_own(i):
        return remote(arg_ref.at[0, pl.ds(0, 2)], kv.at[i, :, x], own_sem, (i,), partner)

    def land_fwd(i):
        return remote(arg_ref.at[0, pl.ds(0, 2)], kv.at[i, :, other], fwd_sem, (i,), partner)

    def land_back(i, block):
        return send_back(i, block)

    rows = 2 * half * tok

    def head_rows(which, head):
        return pl.ds(which * rows + head, tok, stride=2 * half)

    def pack(which, ref):
        stage[which * rows : (which + 1) * rows, :] = ref[...].astype(F32)
        for head in range(2 * half):
            arg_ref[head, which] = stage[head_rows(which, head), :].astype(BF16)

    def unpack(which, head, block):
        stage[head_rows(which, head), :] = block.astype(F32)

    def write(which, ref):
        ref[...] = stage[which * rows : (which + 1) * rows, :].astype(BF16)

    barrier = pltpu.get_barrier_semaphore()
    pl.semaphore_signal(barrier, inc=1, device_id={"seq": partner}, device_id_type=MESH)

    @pl.when(has_next)
    def _():
        pl.semaphore_signal(barrier, inc=1, device_id={"seq": me + 2}, device_id_type=MESH)

    @pl.when(has_prev)
    def _():
        pl.semaphore_signal(barrier, inc=1, device_id={"seq": me - 2}, device_id_type=MESH)

    span_own[...] = jnp.zeros_like(span_own)
    span_own[0:3, :] = spans_ref[...]
    pack(0, key_ref)
    pack(1, value_ref)
    pl.semaphore_wait(barrier, 1 + has_next.astype(jnp.int32) + has_prev.astype(jnp.int32))

    send_spans().start()
    for i in range(half):
        send_kv(i).start()

    @pl.when(has_next)
    def _():
        for i in range(half):
            send_own(i).start()

    pack(2, query_ref)
    pack(3, grad_ref)
    for i in range(half):
        send_qd(i).start()

    @pl.when(jnp.logical_not(has_prev))
    def _():
        for i in range(half):
            for which in range(2):
                kv[i, which, 0:2] = jnp.zeros((2, tok, head_size), BF16)

    @pl.when(jnp.logical_not(has_next))
    def _():
        halo_back[...] = jnp.zeros_like(halo_back)

    for i in range(half):
        kv[i, :, 2 + x] = arg_ref[x * half + i, 0:2]
        qd[i, x] = arg_ref[x * half + i, 2:4]

    send_spans().wait_recv()
    lane = lax.broadcasted_iota(jnp.int32, (1, tok), 1)
    for block in range(2):
        mine = x == block
        start_at = pair * (2 * tok) + block * tok
        low, chosen, rejected = [
            jnp.where(mine, span_own[r : r + 1, :], span_other[r : r + 1, :]) - start_at
            for r in range(3)
        ]
        chosen = jnp.where(lane >= rejected, chosen, 2 * tok)
        for part in range(3):
            at = lax.broadcasted_iota(jnp.int32, (tok, tok), 0) + (part - 2) * tok
            seen = (at >= low) & (at <= lane) & ((at < chosen) | (at >= rejected))
            bias[block, part] = jnp.where(seen, 0.0, NEG)

    def compute(i):
        for block in range(2):
            queries = qd[i, block, 0]
            out_grad = qd[i, block, 1]
            row_max = jnp.full((1, tok), -jnp.inf, F32)
            for part in range(3):
                raw = dot_nt(kv[i, 0, block + part], queries)
                scores = raw * (score_scale * math.log2(math.e)) + bias[block, part]
                s_buf[part] = scores
                row_max = jnp.maximum(row_max, jnp.max(scores, axis=0, keepdims=True))
            row_sum = jnp.zeros((1, tok), F32)
            delta = jnp.zeros((1, tok), F32)
            mixed = jnp.zeros((head_size, tok), F32)
            for part in range(3):
                weights = jnp.exp2(s_buf[part] - row_max)
                row_sum = row_sum + jnp.sum(weights, axis=0, keepdims=True)
                values = kv[i, 1, block + part]
                prob_grad = dot_nt(values, out_grad)
                delta = delta + jnp.sum(weights * prob_grad, axis=0, keepdims=True)
                s_buf[part] = weights
                dp_buf[part] = prob_grad
                mixed = mixed + dot_tn(values, weights.astype(BF16))
            inverse = 1.0 / row_sum
            delta = delta * inverse
            od[i, block, 0] = (mixed * inverse).T.astype(BF16)
            query_grad = jnp.zeros((head_size, tok), F32)
            for part in range(3):
                probs = s_buf[part] * inverse
                score_grad = (probs * (dp_buf[part] - delta)).astype(BF16)
                value_part = dot_nn(probs.astype(BF16), out_grad)
                key_part = dot_nn(score_grad, queries) * score_scale
                query_grad = query_grad + dot_tn(kv[i, 0, block + part], score_grad)
                at = block + part
                if block == 1 and part < 2:
                    key_part = key_part + grads[i, at, 0]
                    value_part = value_part + grads[i, at, 1]
                grads[i, at, 0] = key_part
                grads[i, at, 1] = value_part
            od[i, block, 1] = (query_grad * score_scale).T.astype(BF16)

    def finish(i):
        @pl.when(has_next)
        def _():
            land_back(i, other).wait_recv()

        last[i] = (grads[i, 2 + other] + halo_back[i, other].astype(F32)).astype(BF16)
        send_last(i).start()

        @pl.when(has_next)
        def _():
            land_back(i, x).wait_recv()

        done = grads[i, 2 + x] + halo_back[i, x].astype(F32)
        for which in range(2):
            unpack(2 + which, x * half + i, done[which])

    def step(i, carry):
        land_kv(i).wait_recv()

        @pl.when(has_next)
        def _():
            send_fwd(i).start()

        land_qd(i).wait_recv()

        @pl.when(has_prev)
        def _():
            land_own(i).wait_recv()
            land_fwd(i).wait_recv()

        compute(i)

        @pl.when(has_prev)
        def _():
            halo_out[i] = grads[i, 0:2].astype(BF16)
            send_back(i, other).start()
            send_back(i, x).start()

        send_od(i).start()
        for which in range(2):
            unpack(which, x * half + i, od[i, x, which])

        @pl.when(i > 0)
        def _():
            finish(i - 1)

        return carry

    lax.fori_loop(0, half, step, 0)
    finish(half - 1)

    for i in range(half):
        send_od(i).wait_recv()
        for which in range(2):
            unpack(which, other * half + i, od_in[i, which])
        if i == half - 1:
            write(0, att_out)
            write(1, query_out)
        send_last(i).wait_recv()
        for which in range(2):
            unpack(2 + which, other * half + i, last_in[i, which])
    write(2, key_out)
    write(3, value_out)

    send_spans().wait_send()
    for i in range(half):
        send_kv(i).wait_send()
        send_qd(i).wait_send()
        send_od(i).wait_send()
        send_last(i).wait_send()

    @pl.when(has_next)
    def _():
        for i in range(half):
            send_own(i).wait_send()
            send_fwd(i).wait_send()

    @pl.when(has_prev)
    def _():
        for i in range(half):
            send_back(i, other).wait_send()
            send_back(i, x).wait_send()


def per_device(count, queries, keys, values, out_grad, spans):
    tok, heads, head_size = queries.shape
    half = heads // 2
    flat = [a.reshape(tok * heads, head_size) for a in (keys, values, queries, out_grad)]
    vmem = pltpu.VMEM
    dma = pltpu.SemaphoreType.DMA
    blocks = 3 * 2 * heads // 2
    out = pl.pallas_call(
        functools.partial(kernel, count, tok, half, head_size),
        out_shape=[jax.ShapeDtypeStruct((tok * heads, head_size), BF16)] * 4,
        in_specs=[pl.BlockSpec(memory_space=vmem)] * 5,
        out_specs=[pl.BlockSpec(memory_space=vmem)] * 4,
        scratch_shapes=[
            vmem((heads, 4, tok, head_size), BF16),
            vmem((4 * heads * tok, head_size), F32),
            vmem((half, 2, tok, head_size), BF16),
            vmem((half, 2, tok, head_size), BF16),
            vmem((half, 2, 4, tok, head_size), BF16),
            vmem((half, 2, 2, tok, head_size), BF16),
            vmem((8, tok), jnp.int32),
            vmem((8, tok), jnp.int32),
            vmem((2, 3, tok, tok), F32),
            vmem((3, tok, tok), F32),
            vmem((3, tok, tok), F32),
            vmem((half, 4, 2, tok, head_size), F32),
            vmem((half, 2, 2, tok, head_size), BF16),
            vmem((half, 2, 2, tok, head_size), BF16),
            vmem((half, 2, 2, tok, head_size), BF16),
            vmem((half, 2, tok, head_size), BF16),
            dma((2,)),
            dma((2, half)),
            dma((2, half)),
            dma((2, half)),
            dma((2, half)),
            dma((2, half, 2)),
            dma((2, half)),
            dma((2, half)),
        ],
        compiler_params=pltpu.CompilerParams(
            collective_id=0, has_side_effects=True, vmem_limit_bytes=48 * 1024 * 1024
        ),
        cost_estimate=pl.CostEstimate(
            flops=blocks * 12 * tok * tok * head_size,
            bytes_accessed=16 * heads * tok * head_size,
            transcendentals=blocks * tok * tok,
        ),
    )(*flat, spans)
    return tuple(a.reshape(tok, heads, head_size) for a in out)


def solution(mesh):
    spec = P(("groups", "seq"), "heads", None)
    return jax.shard_map(
        functools.partial(per_device, mesh.shape["seq"]),
        mesh=mesh,
        in_specs=(spec,) * 4 + (P(None, ("groups", "seq")),),
        out_specs=(spec,) * 4,
        check_vma=False,
    )
```

```python
import functools
import math

import jax
import jax.numpy as jnp
from jax import lax
from jax.experimental import pallas as pl
from jax.experimental.pallas import tpu as pltpu
from jax.sharding import PartitionSpec as P

NEG = -1e30
PIECES = 2
MESH = pl.DeviceIdType.MESH
F32 = jnp.float32
BF16 = jnp.bfloat16


def dot_nt(a, b):
    return lax.dot_general(a, b, (((1,), (1,)), ((), ())), preferred_element_type=F32)


def dot_tn(a, b):
    return lax.dot_general(a, b, (((0,), (0,)), ((), ())), preferred_element_type=F32)


def dot_nn(a, b):
    return lax.dot_general(a, b, (((1,), (0,)), ((), ())), preferred_element_type=F32)


def kernel(
    count, tok, half, head_size,
    key_ref, value_ref, query_ref, grad_ref, spans_ref,
    att_out, query_out, key_out, value_out,
    flat, spans_in, arg_ref, stage, od_in, last_in, kv, qd, span_own, span_other, bias, s_buf, dp_buf, grads, halo_out, halo_back, od, last,
    load_sem, span_load_sem, span_sem, kv_sem, qd_sem, own_sem, fwd_sem, back_sem, od_sem, last_sem,
):
    me = lax.axis_index("seq")
    x = lax.rem(me, 2)
    other = 1 - x
    pair = lax.div(me, 2)
    partner = me + 1 - 2 * x
    has_next = me + 2 < count
    has_prev = me >= 2
    score_scale = 1.0 / math.sqrt(head_size)

    def remote(src, dst, sems, at, to):
        return pltpu.make_async_remote_copy(
            src_ref=src,
            dst_ref=dst,
            send_sem=sems.at[(0,) + at],
            recv_sem=sems.at[(1,) + at],
            device_id={"seq": to},
            device_id_type=MESH,
        )

    def send_spans():
        return remote(span_own, span_other, span_sem, (), partner)

    def send_kv(i):
        src = arg_ref.at[other * half + i, pl.ds(0, 2)]
        return remote(src, kv.at[i, :, 2 + x], kv_sem, (i,), partner)

    def send_qd(i):
        src = arg_ref.at[other * half + i, pl.ds(2, 2)]
        return remote(src, qd.at[i, x], qd_sem, (i,), partner)

    def send_own(i):
        src = arg_ref.at[x * half + i, pl.ds(0, 2)]
        return remote(src, kv.at[i, :, x], own_sem, (i,), me + 2)

    def send_fwd(i):
        return remote(kv.at[i, :, 2 + other], kv.at[i, :, other], fwd_sem, (i,), me + 2)

    def send_back(i, block):
        return remote(halo_out.at[i, block], halo_back.at[i, block], back_sem, (i, block), me - 2)

    def send_od(i):
        return remote(od.at[i, other], od_in.at[i], od_sem, (i,), partner)

    def send_last(i):
        return remote(last.at[i], last_in.at[i], last_sem, (i,), partner)

    def land_kv(i):
        dst = kv.at[i, :, 2 + other]
        return remote(arg_ref.at[0, pl.ds(0, 2)], dst, kv_sem, (i,), partner)

    def land_qd(i):
        return remote(arg_ref.at[0, pl.ds(2, 2)], qd.at[i, other], qd_sem, (i,), partner)

    def land_own(i):
        return remote(arg_ref.at[0, pl.ds(0, 2)], kv.at[i, :, x], own_sem, (i,), partner)

    def land_fwd(i):
        return remote(arg_ref.at[0, pl.ds(0, 2)], kv.at[i, :, other], fwd_sem, (i,), partner)

    rows = 2 * half * tok

    def head_rows(which, head):
        return pl.ds(which * rows + head, tok, stride=2 * half)

    def pack(which):
        for piece in range(PIECES):
            load(which, piece).wait()
        stage[which * rows : (which + 1) * rows, :] = flat[which].astype(F32)
        for head in range(2 * half):
            arg_ref[head, which] = stage[head_rows(which, head), :].astype(BF16)

    def unpack(which, head, block):
        stage[head_rows(which, head), :] = block.astype(F32)

    def write(which, ref):
        ref[...] = stage[which * rows : (which + 1) * rows, :].astype(BF16)

    inputs = (key_ref, value_ref, query_ref, grad_ref)

    def load(which, piece):
        at = pl.ds(piece * (rows // PIECES), rows // PIECES)
        return pltpu.make_async_copy(
            inputs[which].at[at], flat.at[which, at], load_sem.at[which, piece]
        )

    load_spans = pltpu.make_async_copy(spans_ref, spans_in, span_load_sem)
    for which in range(4):
        for piece in range(PIECES):
            load(which, piece).start()
    load_spans.start()

    barrier = pltpu.get_barrier_semaphore()
    pl.semaphore_signal(barrier, inc=1, device_id={"seq": partner}, device_id_type=MESH)

    @pl.when(has_next)
    def _():
        pl.semaphore_signal(barrier, inc=1, device_id={"seq": me + 2}, device_id_type=MESH)

    @pl.when(has_prev)
    def _():
        pl.semaphore_signal(barrier, inc=1, device_id={"seq": me - 2}, device_id_type=MESH)

    span_own[...] = jnp.zeros_like(span_own)
    pack(0)
    pack(1)
    load_spans.wait()
    span_own[0:3, :] = spans_in[...]
    pl.semaphore_wait(barrier, 1 + has_next.astype(jnp.int32) + has_prev.astype(jnp.int32))

    send_kv(0).start()

    @pl.when(has_next)
    def _():
        send_own(0).start()
        send_own(1).start()

    send_spans().start()
    pack(2)
    pack(3)
    send_qd(0).start()
    send_kv(1).start()
    send_qd(1).start()

    @pl.when(jnp.logical_not(has_prev))
    def _():
        for i in range(half):
            for which in range(2):
                kv[i, which, 0:2] = jnp.zeros((2, tok, head_size), BF16)

    @pl.when(jnp.logical_not(has_next))
    def _():
        halo_back[...] = jnp.zeros_like(halo_back)

    for i in range(half):
        kv[i, :, 2 + x] = arg_ref[x * half + i, 0:2]
        qd[i, x] = arg_ref[x * half + i, 2:4]

    send_spans().wait_recv()
    lane = lax.broadcasted_iota(jnp.int32, (1, tok), 1)
    for block in range(2):
        mine = x == block
        start_at = pair * (2 * tok) + block * tok
        low, chosen, rejected = [
            jnp.where(mine, span_own[r : r + 1, :], span_other[r : r + 1, :]) - start_at
            for r in range(3)
        ]
        chosen = jnp.where(lane >= rejected, chosen, 2 * tok)
        for part in range(3):
            at = lax.broadcasted_iota(jnp.int32, (tok, tok), 0) + (part - 2) * tok
            seen = (at >= low) & (at <= lane) & ((at < chosen) | (at >= rejected))
            bias[block, part] = jnp.where(seen, 0.0, NEG)

    def compute(i):
        for block in range(2):
            queries = qd[i, block, 0]
            out_grad = qd[i, block, 1]
            row_max = jnp.full((1, tok), -jnp.inf, F32)
            for part in range(3):
                raw = dot_nt(kv[i, 0, block + part], queries)
                scores = raw * (score_scale * math.log2(math.e)) + bias[block, part]
                s_buf[part] = scores
                row_max = jnp.maximum(row_max, jnp.max(scores, axis=0, keepdims=True))
            row_sum = jnp.zeros((1, tok), F32)
            delta = jnp.zeros((1, tok), F32)
            mixed = jnp.zeros((head_size, tok), F32)
            for part in range(3):
                weights = jnp.exp2(s_buf[part] - row_max)
                row_sum = row_sum + jnp.sum(weights, axis=0, keepdims=True)
                values = kv[i, 1, block + part]
                prob_grad = dot_nt(values, out_grad)
                delta = delta + jnp.sum(weights * prob_grad, axis=0, keepdims=True)
                s_buf[part] = weights
                dp_buf[part] = prob_grad
                mixed = mixed + dot_tn(values, weights.astype(BF16))
            inverse = 1.0 / row_sum
            delta = delta * inverse
            od[i, block, 0] = (mixed * inverse).T.astype(BF16)
            query_grad = jnp.zeros((head_size, tok), F32)
            for part in range(3):
                probs = s_buf[part] * inverse
                score_grad = (probs * (dp_buf[part] - delta)).astype(BF16)
                value_part = dot_nn(probs.astype(BF16), out_grad)
                key_part = dot_nn(score_grad, queries) * score_scale
                query_grad = query_grad + dot_tn(kv[i, 0, block + part], score_grad)
                at = block + part
                if block == 1 and part < 2:
                    key_part = key_part + grads[i, at, 0]
                    value_part = value_part + grads[i, at, 1]
                grads[i, at, 0] = key_part
                grads[i, at, 1] = value_part
            od[i, block, 1] = (query_grad * score_scale).T.astype(BF16)

    def total(i, block):
        return (grads[i, 2 + block] + halo_back[i, block].astype(F32)).astype(BF16)

    def finish(i):
        @pl.when(has_next)
        def _():
            send_back(i, other).wait_recv()

        last[i] = total(i, other)
        send_last(i).start()

    def forward(i):
        land_kv(i).wait_recv()

        @pl.when(has_next)
        def _():
            send_fwd(i).start()

    def step(i, carry):
        land_qd(i).wait_recv()

        @pl.when(i + 2 < half)
        def _():
            send_kv(i + 2).start()

        @pl.when(i + 1 < half)
        def _():
            forward(i + 1)

        @pl.when(i + 2 < half)
        def _():
            send_qd(i + 2).start()

            @pl.when(has_next)
            def _():
                send_own(i + 2).start()

        @pl.when(has_prev)
        def _():
            land_own(i).wait_recv()
            land_fwd(i).wait_recv()

        compute(i)

        @pl.when(has_prev)
        def _():
            halo_out[i] = grads[i, 0:2].astype(BF16)
            send_back(i, other).start()
            send_back(i, x).start()

        send_od(i).start()
        for which in range(2):
            unpack(which, x * half + i, od[i, x, which])

        @pl.when(i > 0)
        def _():
            finish(i - 1)

        return carry

    forward(0)
    lax.fori_loop(0, half, step, 0)
    finish(half - 1)

    for i in range(half):
        @pl.when(has_next)
        def _():
            send_back(i, x).wait_recv()

        done = total(i, x)
        for which in range(2):
            unpack(2 + which, x * half + i, done[which])
        send_od(i).wait_recv()
        for which in range(2):
            unpack(which, other * half + i, od_in[i, which])
        if i == half - 1:
            write(0, att_out)
            write(1, query_out)
        send_last(i).wait_recv()
        for which in range(2):
            unpack(2 + which, other * half + i, last_in[i, which])
    write(2, key_out)
    write(3, value_out)

    send_spans().wait_send()
    for i in range(half):
        send_kv(i).wait_send()
        send_qd(i).wait_send()
        send_od(i).wait_send()
        send_last(i).wait_send()

    @pl.when(has_next)
    def _():
        for i in range(half):
            send_own(i).wait_send()
            send_fwd(i).wait_send()

    @pl.when(has_prev)
    def _():
        for i in range(half):
            send_back(i, other).wait_send()
            send_back(i, x).wait_send()


def writer(att_ref, query_ref, key_ref, value_ref, att_out, query_out, key_out, value_out, sems):
    pairs = (
        (att_ref, att_out), (query_ref, query_out), (key_ref, key_out), (value_ref, value_out)
    )
    copies = []
    for which, (src, dst) in enumerate(pairs):
        rows = src.shape[0] // PIECES
        for piece in range(PIECES):
            at = pl.ds(piece * rows, rows)
            copies.append(pltpu.make_async_copy(src.at[at], dst.at[at], sems.at[which, piece]))
    for copy in copies:
        copy.start()
    for copy in copies:
        copy.wait()


def per_device(count, queries, keys, values, out_grad, spans):
    tok, heads, head_size = queries.shape
    half = heads // 2
    flat = [a.reshape(tok * heads, head_size) for a in (keys, values, queries, out_grad)]
    vmem = pltpu.VMEM
    dma = pltpu.SemaphoreType.DMA
    blocks = 3 * 2 * heads // 2
    out = pl.pallas_call(
        functools.partial(kernel, count, tok, half, head_size),
        out_shape=[jax.ShapeDtypeStruct((tok * heads, head_size), BF16)] * 4,
        in_specs=[pl.BlockSpec(memory_space=pltpu.HBM)] * 5,
        out_specs=[pl.BlockSpec(memory_space=vmem)] * 4,
        scratch_shapes=[
            vmem((4, heads * tok, head_size), BF16),
            vmem(spans.shape, jnp.int32),
            vmem((heads, 4, tok, head_size), BF16),
            vmem((4 * heads * tok, head_size), F32),
            vmem((half, 2, tok, head_size), BF16),
            vmem((half, 2, tok, head_size), BF16),
            vmem((half, 2, 4, tok, head_size), BF16),
            vmem((half, 2, 2, tok, head_size), BF16),
            vmem((8, tok), jnp.int32),
            vmem((8, tok), jnp.int32),
            vmem((2, 3, tok, tok), F32),
            vmem((3, tok, tok), F32),
            vmem((3, tok, tok), F32),
            vmem((half, 4, 2, tok, head_size), F32),
            vmem((half, 2, 2, tok, head_size), BF16),
            vmem((half, 2, 2, tok, head_size), BF16),
            vmem((half, 2, 2, tok, head_size), BF16),
            vmem((half, 2, tok, head_size), BF16),
            dma((4, PIECES)),
            dma,
            dma((2,)),
            dma((2, half)),
            dma((2, half)),
            dma((2, half)),
            dma((2, half)),
            dma((2, half, 2)),
            dma((2, half)),
            dma((2, half)),
        ],
        compiler_params=pltpu.CompilerParams(
            collective_id=0, has_side_effects=True, vmem_limit_bytes=52736 * 1024
        ),
        cost_estimate=pl.CostEstimate(
            flops=blocks * 12 * tok * tok * head_size,
            bytes_accessed=8 * heads * tok * head_size,
            transcendentals=blocks * tok * tok,
        ),
    )(*flat, spans)
    out = pl.pallas_call(
        writer,
        out_shape=[jax.ShapeDtypeStruct((tok * heads, head_size), BF16)] * 4,
        in_specs=[pl.BlockSpec(memory_space=vmem)] * 4,
        out_specs=[pl.BlockSpec(memory_space=pltpu.HBM)] * 4,
        scratch_shapes=[dma((4, PIECES))],
    )(*out)
    return tuple(a.reshape(tok, heads, head_size) for a in out)


def solution(mesh):
    spec = P(("groups", "seq"), "heads", None)
    return jax.shard_map(
        functools.partial(per_device, mesh.shape["seq"]),
        mesh=mesh,
        in_specs=(spec,) * 4 + (P(None, ("groups", "seq")),),
        out_specs=(spec,) * 4,
        check_vma=False,
    )
```

```python
import functools
import math

import jax
import jax.numpy as jnp
from jax import lax
from jax.experimental import pallas as pl
from jax.experimental.pallas import tpu as pltpu
from jax.sharding import PartitionSpec as P

NEG = -1e30
PIECES = 2
MESH = pl.DeviceIdType.MESH
F32 = jnp.float32
BF16 = jnp.bfloat16


def dot_nt(a, b):
    return lax.dot_general(a, b, (((1,), (1,)), ((), ())), preferred_element_type=F32)


def dot_tn(a, b):
    return lax.dot_general(a, b, (((0,), (0,)), ((), ())), preferred_element_type=F32)


def dot_nn(a, b):
    return lax.dot_general(a, b, (((1,), (0,)), ((), ())), preferred_element_type=F32)


def kernel(
    count, tok, half, head_size,
    key_ref, value_ref, query_ref, grad_ref, spans_ref,
    att_out, query_out, key_out, value_out,
    flat, spans_in, arg_ref, stage, od_in, last_in, kv, qd, span_own, span_other, bias, s_buf, dp_buf, grads, halo_out, halo_back, od, last,
    load_sem, span_load_sem, span_sem, kv_sem, qd_sem, own_sem, fwd_sem, back_sem, od_sem, last_sem,
):
    me = lax.axis_index("seq")
    x = lax.rem(me, 2)
    other = 1 - x
    pair = lax.div(me, 2)
    partner = me + 1 - 2 * x
    has_next = me + 2 < count
    has_prev = me >= 2
    score_scale = 1.0 / math.sqrt(head_size)

    def remote(src, dst, sems, at, to):
        return pltpu.make_async_remote_copy(
            src_ref=src,
            dst_ref=dst,
            send_sem=sems.at[(0,) + at],
            recv_sem=sems.at[(1,) + at],
            device_id={"seq": to},
            device_id_type=MESH,
        )

    def send_spans():
        return remote(span_own, span_other, span_sem, (), partner)

    def send_kv(i):
        src = arg_ref.at[other * half + i, pl.ds(0, 2)]
        return remote(src, kv.at[i, :, 2 + x], kv_sem, (i,), partner)

    def send_qd(i):
        src = arg_ref.at[other * half + i, pl.ds(2, 2)]
        return remote(src, qd.at[i, x], qd_sem, (i,), partner)

    def send_own(i):
        src = arg_ref.at[x * half + i, pl.ds(0, 2)]
        return remote(src, kv.at[i, :, x], own_sem, (i,), me + 2)

    def send_fwd(i):
        return remote(kv.at[i, :, 2 + other], kv.at[i, :, other], fwd_sem, (i,), me + 2)

    def send_back(i, block):
        return remote(halo_out.at[i, block], halo_back.at[i, block], back_sem, (i, block), me - 2)

    def send_od(i):
        return remote(od.at[i, other], od_in.at[i], od_sem, (i,), partner)

    def send_last(i):
        return remote(last.at[i], last_in.at[i], last_sem, (i,), partner)

    def land_kv(i):
        dst = kv.at[i, :, 2 + other]
        return remote(arg_ref.at[0, pl.ds(0, 2)], dst, kv_sem, (i,), partner)

    def land_qd(i):
        return remote(arg_ref.at[0, pl.ds(2, 2)], qd.at[i, other], qd_sem, (i,), partner)

    def land_own(i):
        return remote(arg_ref.at[0, pl.ds(0, 2)], kv.at[i, :, x], own_sem, (i,), partner)

    def land_fwd(i):
        return remote(arg_ref.at[0, pl.ds(0, 2)], kv.at[i, :, other], fwd_sem, (i,), partner)

    rows = 2 * half * tok

    def head_rows(which, head):
        return pl.ds(which * rows + head, tok, stride=2 * half)

    def pack(which):
        for piece in range(PIECES):
            load(which, piece).wait()
        stage[which * rows : (which + 1) * rows, :] = flat[which].astype(F32)
        for head in range(2 * half):
            arg_ref[head, which] = stage[head_rows(which, head), :].astype(BF16)

    def unpack(which, head, block):
        stage[head_rows(which, head), :] = block.astype(F32)

    def write(which, ref):
        ref[...] = stage[which * rows : (which + 1) * rows, :].astype(BF16)

    inputs = (key_ref, value_ref, query_ref, grad_ref)

    def load(which, piece):
        at = pl.ds(piece * (rows // PIECES), rows // PIECES)
        return pltpu.make_async_copy(
            inputs[which].at[at], flat.at[which, at], load_sem.at[which, piece]
        )

    load_spans = pltpu.make_async_copy(spans_ref, spans_in, span_load_sem)
    for which in range(4):
        for piece in range(PIECES):
            load(which, piece).start()
    load_spans.start()

    barrier = pltpu.get_barrier_semaphore()
    pl.semaphore_signal(barrier, inc=1, device_id={"seq": partner}, device_id_type=MESH)

    @pl.when(has_next)
    def _():
        pl.semaphore_signal(barrier, inc=1, device_id={"seq": me + 2}, device_id_type=MESH)

    @pl.when(has_prev)
    def _():
        pl.semaphore_signal(barrier, inc=1, device_id={"seq": me - 2}, device_id_type=MESH)

    span_own[...] = jnp.zeros_like(span_own)
    pack(0)
    pack(1)
    load_spans.wait()
    span_own[0:3, :] = spans_in[...]
    pl.semaphore_wait(barrier, 1 + has_next.astype(jnp.int32) + has_prev.astype(jnp.int32))

    send_kv(0).start()

    @pl.when(has_next)
    def _():
        send_own(0).start()
        send_own(1).start()

    send_spans().start()
    pack(2)
    pack(3)
    send_qd(0).start()
    send_kv(1).start()
    send_qd(1).start()

    @pl.when(jnp.logical_not(has_prev))
    def _():
        for i in range(half):
            for which in range(2):
                kv[i, which, 0:2] = jnp.zeros((2, tok, head_size), BF16)

    @pl.when(jnp.logical_not(has_next))
    def _():
        halo_back[...] = jnp.zeros_like(halo_back)

    for i in range(half):
        kv[i, :, 2 + x] = arg_ref[x * half + i, 0:2]
        qd[i, x] = arg_ref[x * half + i, 2:4]

    send_spans().wait_recv()
    lane = lax.broadcasted_iota(jnp.int32, (1, tok), 1)
    for block in range(2):
        mine = x == block
        start_at = pair * (2 * tok) + block * tok
        low, chosen, rejected = [
            jnp.where(mine, span_own[r : r + 1, :], span_other[r : r + 1, :]) - start_at
            for r in range(3)
        ]
        chosen = jnp.where(lane >= rejected, chosen, 2 * tok)
        for part in range(3):
            at = lax.broadcasted_iota(jnp.int32, (tok, tok), 0) + (part - 2) * tok
            seen = (at >= low) & (at <= lane) & ((at < chosen) | (at >= rejected))
            bias[block, part] = jnp.where(seen, 0.0, NEG)

    def compute(i):
        for block in range(2):
            queries = qd[i, block, 0]
            out_grad = qd[i, block, 1]
            row_max = jnp.full((1, tok), -jnp.inf, F32)
            for part in range(3):
                raw = dot_nt(kv[i, 0, block + part], queries)
                scores = raw * (score_scale * math.log2(math.e)) + bias[block, part]
                s_buf[part] = scores
                row_max = jnp.maximum(row_max, jnp.max(scores, axis=0, keepdims=True))
            row_sum = jnp.zeros((1, tok), F32)
            delta = jnp.zeros((1, tok), F32)
            mixed = jnp.zeros((head_size, tok), F32)
            for part in range(3):
                weights = jnp.exp2(s_buf[part] - row_max)
                row_sum = row_sum + jnp.sum(weights, axis=0, keepdims=True)
                values = kv[i, 1, block + part]
                prob_grad = dot_nt(values, out_grad)
                delta = delta + jnp.sum(weights * prob_grad, axis=0, keepdims=True)
                s_buf[part] = weights
                dp_buf[part] = prob_grad
                mixed = mixed + dot_tn(values, weights.astype(BF16))
            inverse = 1.0 / row_sum
            delta = delta * inverse
            od[i, block, 0] = (mixed * inverse).T.astype(BF16)
            query_grad = jnp.zeros((head_size, tok), F32)
            for part in range(3):
                probs = s_buf[part] * inverse
                score_grad = (probs * (dp_buf[part] - delta)).astype(BF16)
                value_part = dot_nn(probs.astype(BF16), out_grad)
                key_part = dot_nn(score_grad, queries) * score_scale
                query_grad = query_grad + dot_tn(kv[i, 0, block + part], score_grad)
                at = block + part
                if block == 1 and part < 2:
                    key_part = key_part + grads[i, at, 0]
                    value_part = value_part + grads[i, at, 1]
                grads[i, at, 0] = key_part
                grads[i, at, 1] = value_part
            od[i, block, 1] = (query_grad * score_scale).T.astype(BF16)

    def total(i, block):
        return (grads[i, 2 + block] + halo_back[i, block].astype(F32)).astype(BF16)

    def finish(i):
        @pl.when(has_next)
        def _():
            send_back(i, other).wait_recv()

        last[i] = total(i, other)
        send_last(i).start()

    def forward(i):
        land_kv(i).wait_recv()

        @pl.when(has_next)
        def _():
            send_fwd(i).start()

    def step(i, carry):
        land_qd(i).wait_recv()

        @pl.when(i + 2 < half)
        def _():
            send_kv(i + 2).start()

        @pl.when(i + 1 < half)
        def _():
            forward(i + 1)

        @pl.when(i + 2 < half)
        def _():
            send_qd(i + 2).start()

            @pl.when(has_next)
            def _():
                send_own(i + 2).start()

        @pl.when(has_prev)
        def _():
            land_own(i).wait_recv()
            land_fwd(i).wait_recv()

        compute(i)

        @pl.when(has_prev)
        def _():
            halo_out[i] = grads[i, 0:2].astype(BF16)
            send_back(i, other).start()
            send_back(i, x).start()

        send_od(i).start()
        for which in range(2):
            unpack(which, x * half + i, od[i, x, which])

        @pl.when(i > 0)
        def _():
            finish(i - 1)

        return carry

    forward(0)
    lax.fori_loop(0, half, step, 0)
    finish(half - 1)

    for i in range(half):
        @pl.when(has_next)
        def _():
            send_back(i, x).wait_recv()

        done = total(i, x)
        for which in range(2):
            unpack(2 + which, x * half + i, done[which])
        send_od(i).wait_recv()
        for which in range(2):
            unpack(which, other * half + i, od_in[i, which])
        if i == half - 1:
            write(0, att_out)
            write(1, query_out)
        send_last(i).wait_recv()
        for which in range(2):
            unpack(2 + which, other * half + i, last_in[i, which])
    write(2, key_out)
    write(3, value_out)

    send_spans().wait_send()
    for i in range(half):
        send_kv(i).wait_send()
        send_qd(i).wait_send()
        send_od(i).wait_send()
        send_last(i).wait_send()

    @pl.when(has_next)
    def _():
        for i in range(half):
            send_own(i).wait_send()
            send_fwd(i).wait_send()

    @pl.when(has_prev)
    def _():
        for i in range(half):
            send_back(i, other).wait_send()
            send_back(i, x).wait_send()


def per_device(count, queries, keys, values, out_grad, spans):
    tok, heads, head_size = queries.shape
    half = heads // 2
    flat = [a.reshape(tok * heads, head_size) for a in (keys, values, queries, out_grad)]
    vmem = pltpu.VMEM
    dma = pltpu.SemaphoreType.DMA
    blocks = 3 * 2 * heads // 2
    out = pl.pallas_call(
        functools.partial(kernel, count, tok, half, head_size),
        out_shape=[vmem((tok * heads, head_size), BF16)] * 4,
        in_specs=[pl.BlockSpec(memory_space=pltpu.HBM)] * 5,
        out_specs=[pl.BlockSpec(memory_space=vmem)] * 4,
        scratch_shapes=[
            vmem((4, heads * tok, head_size), BF16),
            vmem(spans.shape, jnp.int32),
            vmem((heads, 4, tok, head_size), BF16),
            vmem((4 * heads * tok, head_size), F32),
            vmem((half, 2, tok, head_size), BF16),
            vmem((half, 2, tok, head_size), BF16),
            vmem((half, 2, 4, tok, head_size), BF16),
            vmem((half, 2, 2, tok, head_size), BF16),
            vmem((8, tok), jnp.int32),
            vmem((8, tok), jnp.int32),
            vmem((2, 3, tok, tok), F32),
            vmem((3, tok, tok), F32),
            vmem((3, tok, tok), F32),
            vmem((half, 4, 2, tok, head_size), F32),
            vmem((half, 2, 2, tok, head_size), BF16),
            vmem((half, 2, 2, tok, head_size), BF16),
            vmem((half, 2, 2, tok, head_size), BF16),
            vmem((half, 2, tok, head_size), BF16),
            dma((4, PIECES)),
            dma,
            dma((2,)),
            dma((2, half)),
            dma((2, half)),
            dma((2, half)),
            dma((2, half)),
            dma((2, half, 2)),
            dma((2, half)),
            dma((2, half)),
        ],
        compiler_params=pltpu.CompilerParams(
            collective_id=0, has_side_effects=True, vmem_limit_bytes=48 * 1024 * 1024
        ),
        cost_estimate=pl.CostEstimate(
            flops=blocks * 12 * tok * tok * head_size,
            bytes_accessed=8 * heads * tok * head_size,
            transcendentals=blocks * tok * tok,
        ),
    )(*[pltpu.with_memory_space_constraint(a, pltpu.HBM) for a in (*flat, spans)])
    return tuple(a.reshape(tok, heads, head_size) for a in out)


def solution(mesh):
    spec = P(("groups", "seq"), "heads", None)
    return jax.shard_map(
        functools.partial(per_device, mesh.shape["seq"]),
        mesh=mesh,
        in_specs=(spec,) * 4 + (P(None, ("groups", "seq")),),
        out_specs=(spec,) * 4,
        check_vma=False,
    )
```

```python
import functools
import math

import jax
import jax.numpy as jnp
from jax import lax
from jax.experimental import pallas as pl
from jax.experimental.pallas import tpu as pltpu
from jax.sharding import PartitionSpec as P

NEG = -1e30
PIECES = 2
MESH = pl.DeviceIdType.MESH
F32 = jnp.float32
BF16 = jnp.bfloat16


def dot_nt(a, b):
    return lax.dot_general(a, b, (((1,), (1,)), ((), ())), preferred_element_type=F32)


def dot_tn(a, b):
    return lax.dot_general(a, b, (((0,), (0,)), ((), ())), preferred_element_type=F32)


def dot_nn(a, b):
    return lax.dot_general(a, b, (((1,), (0,)), ((), ())), preferred_element_type=F32)


def kernel(
    count, tok, half, head_size,
    key_ref, value_ref, query_ref, grad_ref, spans_ref,
    att_out, query_out, key_out, value_out,
    flat, spans_in, arg_ref, stage, od_in, last_in, kv, qd, span_own, span_other, bias, s_buf, dp_buf, grads, halo_out, halo_back, od, last,
    load_sem, span_load_sem, span_sem, kv_sem, qd_sem, own_sem, fwd_sem, back_sem, od_sem, last_sem,
):
    me = lax.axis_index("seq")
    x = lax.rem(me, 2)
    other = 1 - x
    pair = lax.div(me, 2)
    partner = me + 1 - 2 * x
    has_next = me + 2 < count
    has_prev = me >= 2
    score_scale = 1.0 / math.sqrt(head_size)

    def remote(src, dst, sems, at, to):
        return pltpu.make_async_remote_copy(
            src_ref=src,
            dst_ref=dst,
            send_sem=sems.at[(0,) + at],
            recv_sem=sems.at[(1,) + at],
            device_id={"seq": to},
            device_id_type=MESH,
        )

    def send_spans():
        return remote(span_own, span_other, span_sem, (), partner)

    def send_kv(i):
        src = arg_ref.at[other * half + i, pl.ds(0, 2)]
        return remote(src, kv.at[i, :, 2 + x], kv_sem, (i,), partner)

    def send_qd(i):
        src = arg_ref.at[other * half + i, pl.ds(2, 2)]
        return remote(src, qd.at[i, x], qd_sem, (i,), partner)

    def send_own(i):
        src = arg_ref.at[x * half + i, pl.ds(0, 2)]
        return remote(src, kv.at[i, :, x], own_sem, (i,), me + 2)

    def send_fwd(i):
        return remote(kv.at[i, :, 2 + other], kv.at[i, :, other], fwd_sem, (i,), me + 2)

    def send_back(i, block):
        return remote(halo_out.at[i, block], halo_back.at[i, block], back_sem, (i, block), me - 2)

    def send_od(i):
        return remote(od.at[i, other], od_in.at[i], od_sem, (i,), partner)

    def send_last(i):
        return remote(last.at[i], last_in.at[i], last_sem, (i,), partner)

    def land_kv(i):
        dst = kv.at[i, :, 2 + other]
        return remote(arg_ref.at[0, pl.ds(0, 2)], dst, kv_sem, (i,), partner)

    def land_qd(i):
        return remote(arg_ref.at[0, pl.ds(2, 2)], qd.at[i, other], qd_sem, (i,), partner)

    def land_own(i):
        return remote(arg_ref.at[0, pl.ds(0, 2)], kv.at[i, :, x], own_sem, (i,), partner)

    def land_fwd(i):
        return remote(arg_ref.at[0, pl.ds(0, 2)], kv.at[i, :, other], fwd_sem, (i,), partner)

    rows = 2 * half * tok

    def head_rows(which, head):
        return pl.ds(which * rows + head, tok, stride=2 * half)

    def pack(which, piece):
        span, part = rows // PIECES, tok // PIECES
        low = which * rows + piece * span
        stage[low : low + span, :] = flat[which, piece * span : (piece + 1) * span].astype(F32)
        for head in range(2 * half):
            block = stage[pl.ds(low + head, part, stride=2 * half), :]
            arg_ref[head, which, piece * part : (piece + 1) * part] = block.astype(BF16)

    def unpack(which, head, block):
        stage[head_rows(which, head), :] = block.astype(F32)

    def write(which, ref):
        ref[...] = stage[which * rows : (which + 1) * rows, :].astype(BF16)

    inputs = (key_ref, value_ref, query_ref, grad_ref)

    def load(which, piece):
        at = pl.ds(piece * (rows // PIECES), rows // PIECES)
        return pltpu.make_async_copy(
            inputs[which].at[at], flat.at[which, at], load_sem.at[which, piece]
        )

    load_spans = pltpu.make_async_copy(spans_ref, spans_in, span_load_sem)
    for piece in range(PIECES):
        load(0, piece).start()
        load(1, piece).start()
    load_spans.start()

    barrier = pltpu.get_barrier_semaphore()
    pl.semaphore_signal(barrier, inc=1, device_id={"seq": partner}, device_id_type=MESH)

    @pl.when(has_next)
    def _():
        pl.semaphore_signal(barrier, inc=1, device_id={"seq": me + 2}, device_id_type=MESH)

    @pl.when(has_prev)
    def _():
        pl.semaphore_signal(barrier, inc=1, device_id={"seq": me - 2}, device_id_type=MESH)

    span_own[...] = jnp.zeros_like(span_own)
    for piece in range(PIECES):
        load(0, piece).wait()
        load(1, piece).wait()
        if piece == PIECES - 1:
            for later in range(PIECES):
                load(2, later).start()
                load(3, later).start()
        pack(0, piece)
        pack(1, piece)
    load_spans.wait()
    span_own[0:3, :] = spans_in[...]
    pl.semaphore_wait(barrier, 1 + has_next.astype(jnp.int32) + has_prev.astype(jnp.int32))

    send_kv(0).start()

    @pl.when(has_next)
    def _():
        send_own(0).start()
        send_own(1).start()

    send_spans().start()
    for piece in range(PIECES):
        load(2, piece).wait()
        load(3, piece).wait()
        pack(2, piece)
        pack(3, piece)
    send_qd(0).start()
    send_kv(1).start()
    send_qd(1).start()

    @pl.when(jnp.logical_not(has_prev))
    def _():
        for i in range(half):
            for which in range(2):
                kv[i, which, 0:2] = jnp.zeros((2, tok, head_size), BF16)

    @pl.when(jnp.logical_not(has_next))
    def _():
        halo_back[...] = jnp.zeros_like(halo_back)

    for i in range(half):
        kv[i, :, 2 + x] = arg_ref[x * half + i, 0:2]
        qd[i, x] = arg_ref[x * half + i, 2:4]

    send_spans().wait_recv()
    lane = lax.broadcasted_iota(jnp.int32, (1, tok), 1)
    for block in range(2):
        mine = x == block
        start_at = pair * (2 * tok) + block * tok
        low, chosen, rejected = [
            jnp.where(mine, span_own[r : r + 1, :], span_other[r : r + 1, :]) - start_at
            for r in range(3)
        ]
        chosen = jnp.where(lane >= rejected, chosen, 2 * tok)
        for part in range(3):
            at = lax.broadcasted_iota(jnp.int32, (tok, tok), 0) + (part - 2) * tok
            seen = (at >= low) & (at <= lane) & ((at < chosen) | (at >= rejected))
            bias[block, part] = jnp.where(seen, 0.0, NEG)

    def compute(i):
        for block in range(2):
            queries = qd[i, block, 0]
            out_grad = qd[i, block, 1]
            row_max = jnp.full((1, tok), -jnp.inf, F32)
            for part in range(3):
                raw = dot_nt(kv[i, 0, block + part], queries)
                scores = raw * (score_scale * math.log2(math.e)) + bias[block, part]
                s_buf[part] = scores
                row_max = jnp.maximum(row_max, jnp.max(scores, axis=0, keepdims=True))
            row_sum = jnp.zeros((1, tok), F32)
            delta = jnp.zeros((1, tok), F32)
            mixed = jnp.zeros((head_size, tok), F32)
            for part in range(3):
                weights = jnp.exp2(s_buf[part] - row_max)
                row_sum = row_sum + jnp.sum(weights, axis=0, keepdims=True)
                values = kv[i, 1, block + part]
                prob_grad = dot_nt(values, out_grad)
                delta = delta + jnp.sum(weights * prob_grad, axis=0, keepdims=True)
                s_buf[part] = weights
                dp_buf[part] = prob_grad
                mixed = mixed + dot_tn(values, weights.astype(BF16))
            inverse = 1.0 / row_sum
            delta = delta * inverse
            od[i, block, 0] = (mixed * inverse).T.astype(BF16)
            query_grad = jnp.zeros((head_size, tok), F32)
            for part in range(3):
                probs = s_buf[part] * inverse
                score_grad = (probs * (dp_buf[part] - delta)).astype(BF16)
                value_part = dot_nn(probs.astype(BF16), out_grad)
                key_part = dot_nn(score_grad, queries) * score_scale
                query_grad = query_grad + dot_tn(kv[i, 0, block + part], score_grad)
                at = block + part
                if block == 1 and part < 2:
                    key_part = key_part + grads[i, at, 0]
                    value_part = value_part + grads[i, at, 1]
                grads[i, at, 0] = key_part
                grads[i, at, 1] = value_part
            od[i, block, 1] = (query_grad * score_scale).T.astype(BF16)

    def total(i, block):
        return (grads[i, 2 + block] + halo_back[i, block].astype(F32)).astype(BF16)

    def finish(i):
        @pl.when(has_next)
        def _():
            send_back(i, other).wait_recv()

        last[i] = total(i, other)
        send_last(i).start()

    def forward(i):
        land_kv(i).wait_recv()

        @pl.when(has_next)
        def _():
            send_fwd(i).start()

    def step(i, carry):
        land_qd(i).wait_recv()

        @pl.when(i + 2 < half)
        def _():
            send_kv(i + 2).start()

        @pl.when(i + 1 < half)
        def _():
            forward(i + 1)

        @pl.when(i + 2 < half)
        def _():
            send_qd(i + 2).start()

            @pl.when(has_next)
            def _():
                send_own(i + 2).start()

        @pl.when(has_prev)
        def _():
            land_own(i).wait_recv()
            land_fwd(i).wait_recv()

        @pl.when(i == half - 2)
        def _():
            send_od(0).start()

        compute(i)

        @pl.when(has_prev)
        def _():
            halo_out[i] = grads[i, 0:2].astype(BF16)
            send_back(i, other).start()
            send_back(i, x).start()

        @pl.when(i == half - 2)
        def _():
            for done in range(1, half - 1):
                send_od(done).start()
            for done in range(half - 2):
                finish(done)

        @pl.when(i == half - 1)
        def _():
            send_od(half - 1).start()
            finish(half - 2)

        for which in range(2):
            unpack(which, x * half + i, od[i, x, which])
        return carry

    forward(0)
    lax.fori_loop(0, half, step, 0)
    finish(half - 1)

    for i in range(half):
        @pl.when(has_next)
        def _():
            send_back(i, x).wait_recv()

        done = total(i, x)
        for which in range(2):
            unpack(2 + which, x * half + i, done[which])
        send_od(i).wait_recv()
        for which in range(2):
            unpack(which, other * half + i, od_in[i, which])
        if i == half - 1:
            write(0, att_out)
            write(1, query_out)
        send_last(i).wait_recv()
        for which in range(2):
            unpack(2 + which, other * half + i, last_in[i, which])
    write(2, key_out)
    write(3, value_out)

    send_spans().wait_send()
    for i in range(half):
        send_kv(i).wait_send()
        send_qd(i).wait_send()
        send_od(i).wait_send()
        send_last(i).wait_send()

    @pl.when(has_next)
    def _():
        for i in range(half):
            send_own(i).wait_send()
            send_fwd(i).wait_send()

    @pl.when(has_prev)
    def _():
        for i in range(half):
            send_back(i, other).wait_send()
            send_back(i, x).wait_send()


def per_device(count, queries, keys, values, out_grad, spans):
    tok, heads, head_size = queries.shape
    half = heads // 2
    flat = [a.reshape(tok * heads, head_size) for a in (keys, values, queries, out_grad)]
    vmem = pltpu.VMEM
    dma = pltpu.SemaphoreType.DMA
    blocks = 3 * 2 * heads // 2
    out = pl.pallas_call(
        functools.partial(kernel, count, tok, half, head_size),
        out_shape=[vmem((tok * heads, head_size), BF16)] * 4,
        in_specs=[pl.BlockSpec(memory_space=pltpu.HBM)] * 5,
        out_specs=[pl.BlockSpec(memory_space=vmem)] * 4,
        scratch_shapes=[
            vmem((4, heads * tok, head_size), BF16),
            vmem(spans.shape, jnp.int32),
            vmem((heads, 4, tok, head_size), BF16),
            vmem((4 * heads * tok, head_size), F32),
            vmem((half, 2, tok, head_size), BF16),
            vmem((half, 2, tok, head_size), BF16),
            vmem((half, 2, 4, tok, head_size), BF16),
            vmem((half, 2, 2, tok, head_size), BF16),
            vmem((8, tok), jnp.int32),
            vmem((8, tok), jnp.int32),
            vmem((2, 3, tok, tok), F32),
            vmem((3, tok, tok), F32),
            vmem((3, tok, tok), F32),
            vmem((half, 4, 2, tok, head_size), F32),
            vmem((half, 2, 2, tok, head_size), BF16),
            vmem((half, 2, 2, tok, head_size), BF16),
            vmem((half, 2, 2, tok, head_size), BF16),
            vmem((half, 2, tok, head_size), BF16),
            dma((4, PIECES)),
            dma,
            dma((2,)),
            dma((2, half)),
            dma((2, half)),
            dma((2, half)),
            dma((2, half)),
            dma((2, half, 2)),
            dma((2, half)),
            dma((2, half)),
        ],
        compiler_params=pltpu.CompilerParams(
            collective_id=0, has_side_effects=True, vmem_limit_bytes=48 * 1024 * 1024
        ),
        cost_estimate=pl.CostEstimate(
            flops=blocks * 12 * tok * tok * head_size,
            bytes_accessed=8 * heads * tok * head_size,
            transcendentals=blocks * tok * tok,
        ),
    )(*[pltpu.with_memory_space_constraint(a, pltpu.HBM) for a in (*flat, spans)])
    return tuple(a.reshape(tok, heads, head_size) for a in out)


def solution(mesh):
    spec = P(("groups", "seq"), "heads", None)
    return jax.shard_map(
        functools.partial(per_device, mesh.shape["seq"]),
        mesh=mesh,
        in_specs=(spec,) * 4 + (P(None, ("groups", "seq")),),
        out_specs=(spec,) * 4,
        check_vma=False,
    )
```

```python
import functools
import math

import jax
import jax.numpy as jnp
from jax import lax
from jax.experimental import pallas as pl
from jax.experimental.pallas import tpu as pltpu
from jax.sharding import PartitionSpec as P

NEG = -1e30
PIECES = 2
MESH = pl.DeviceIdType.MESH
F32 = jnp.float32
BF16 = jnp.bfloat16


def dot_nt(a, b):
    return lax.dot_general(a, b, (((1,), (1,)), ((), ())), preferred_element_type=F32)


def dot_tn(a, b):
    return lax.dot_general(a, b, (((0,), (0,)), ((), ())), preferred_element_type=F32)


def dot_nn(a, b):
    return lax.dot_general(a, b, (((1,), (0,)), ((), ())), preferred_element_type=F32)


def kernel(
    count, tok, half, head_size,
    key_ref, value_ref, query_ref, grad_ref, spans_ref,
    out_ref,
    flat, spans_in, arg_ref, stage, od_in, last_in, kv, qd, span_own, span_other, bias, s_buf, dp_buf, grads, halo_out, halo_back, od, last,
    load_sem, span_load_sem, span_sem, kv_sem, qd_sem, own_sem, fwd_sem, back_sem, od_sem, last_sem,
):
    me = lax.axis_index("seq")
    x = lax.rem(me, 2)
    other = 1 - x
    pair = lax.div(me, 2)
    partner = me + 1 - 2 * x
    has_next = me + 2 < count
    has_prev = me >= 2
    score_scale = 1.0 / math.sqrt(head_size)

    def remote(src, dst, sems, at, to):
        return pltpu.make_async_remote_copy(
            src_ref=src,
            dst_ref=dst,
            send_sem=sems.at[(0,) + at],
            recv_sem=sems.at[(1,) + at],
            device_id={"seq": to},
            device_id_type=MESH,
        )

    def send_spans():
        return remote(span_own, span_other, span_sem, (), partner)

    def send_kv(i, which):
        src = arg_ref.at[other * half + i, which]
        return remote(src, kv.at[i, which, 2 + x], kv_sem, (i, which), partner)

    def send_qd(i):
        src = arg_ref.at[other * half + i, pl.ds(2, 2)]
        return remote(src, qd.at[i, x], qd_sem, (i,), partner)

    def send_own(i):
        src = arg_ref.at[x * half + i, pl.ds(0, 2)]
        return remote(src, kv.at[i, :, x], own_sem, (i,), me + 2)

    def send_fwd(i):
        return remote(kv.at[i, :, 2 + other], kv.at[i, :, other], fwd_sem, (i,), me + 2)

    def send_back(i, block):
        return remote(halo_out.at[i, block], halo_back.at[i, block], back_sem, (i, block), me - 2)

    def send_od(i):
        return remote(od.at[i, other], od_in.at[i], od_sem, (i,), partner)

    def send_last(i):
        return remote(last.at[i], last_in.at[i], last_sem, (i,), partner)

    def land_kv(i, which):
        dst = kv.at[i, which, 2 + other]
        return remote(arg_ref.at[0, which], dst, kv_sem, (i, which), partner)

    def land_qd(i):
        return remote(arg_ref.at[0, pl.ds(2, 2)], qd.at[i, other], qd_sem, (i,), partner)

    def land_own(i):
        return remote(arg_ref.at[0, pl.ds(0, 2)], kv.at[i, :, x], own_sem, (i,), partner)

    def land_fwd(i):
        return remote(arg_ref.at[0, pl.ds(0, 2)], kv.at[i, :, other], fwd_sem, (i,), partner)

    rows = 2 * half * tok

    def head_rows(which, head):
        return pl.ds(which * rows + head, tok, stride=2 * half)

    def pack(which, piece):
        span, part = rows // PIECES, tok // PIECES
        low = which * rows + piece * span
        stage[low : low + span, :] = flat[which, piece * span : (piece + 1) * span].astype(F32)
        for head in range(2 * half):
            block = stage[pl.ds(low + head, part, stride=2 * half), :]
            arg_ref[head, which, piece * part : (piece + 1) * part] = block.astype(BF16)

    def unpack(which, head, block):
        stage[head_rows(which, head), :] = block.astype(F32)

    def write(which):
        out_ref[which] = stage[which * rows : (which + 1) * rows, :].astype(BF16)

    inputs = (key_ref, value_ref, query_ref, grad_ref)

    def load(which, piece):
        at = pl.ds(piece * (rows // PIECES), rows // PIECES)
        return pltpu.make_async_copy(
            inputs[which].at[at], flat.at[which, at], load_sem.at[which, piece]
        )

    load_spans = pltpu.make_async_copy(spans_ref, spans_in, span_load_sem)
    for piece in range(PIECES):
        load(0, piece).start()
    for piece in range(PIECES):
        load(1, piece).start()
    load_spans.start()

    barrier = pltpu.get_barrier_semaphore()
    pl.semaphore_signal(barrier, inc=1, device_id={"seq": partner}, device_id_type=MESH)

    @pl.when(has_next)
    def _():
        pl.semaphore_signal(barrier, inc=1, device_id={"seq": me + 2}, device_id_type=MESH)

    @pl.when(has_prev)
    def _():
        pl.semaphore_signal(barrier, inc=1, device_id={"seq": me - 2}, device_id_type=MESH)

    for piece in range(PIECES):
        load(0, piece).wait()
        pack(0, piece)
    pl.semaphore_wait(barrier, 1 + has_next.astype(jnp.int32) + has_prev.astype(jnp.int32))
    send_kv(0, 0).start()
    send_kv(1, 0).start()

    for which in (2, 3):
        for piece in range(PIECES):
            load(which, piece).start()
    for piece in range(PIECES):
        load(1, piece).wait()
        pack(1, piece)
    send_kv(0, 1).start()
    send_kv(1, 1).start()

    @pl.when(has_next)
    def _():
        send_own(0).start()
        send_own(1).start()

    load_spans.wait()
    span_own[...] = jnp.zeros_like(span_own)
    span_own[0:3, :] = spans_in[...]
    send_spans().start()
    for piece in range(PIECES):
        load(2, piece).wait()
        pack(2, piece)
    for piece in range(PIECES):
        load(3, piece).wait()
        pack(3, piece)
    send_qd(0).start()
    send_qd(1).start()

    @pl.when(jnp.logical_not(has_prev))
    def _():
        for i in range(half):
            for which in range(2):
                kv[i, which, 0:2] = jnp.zeros((2, tok, head_size), BF16)

    @pl.when(jnp.logical_not(has_next))
    def _():
        halo_back[...] = jnp.zeros_like(halo_back)

    for i in range(half):
        kv[i, :, 2 + x] = arg_ref[x * half + i, 0:2]
        qd[i, x] = arg_ref[x * half + i, 2:4]

    send_spans().wait_recv()
    lane = lax.broadcasted_iota(jnp.int32, (1, tok), 1)
    for block in range(2):
        mine = x == block
        start_at = pair * (2 * tok) + block * tok
        low, chosen, rejected = [
            jnp.where(mine, span_own[r : r + 1, :], span_other[r : r + 1, :]) - start_at
            for r in range(3)
        ]
        chosen = jnp.where(lane >= rejected, chosen, 2 * tok)
        for part in range(3):
            at = lax.broadcasted_iota(jnp.int32, (tok, tok), 0) + (part - 2) * tok
            seen = (at >= low) & (at <= lane) & ((at < chosen) | (at >= rejected))
            bias[block, part] = jnp.where(seen, 0.0, NEG)

    def compute(i):
        for block in range(2):
            queries = qd[i, block, 0]
            out_grad = qd[i, block, 1]
            row_max = jnp.full((1, tok), -jnp.inf, F32)
            for part in range(3):
                raw = dot_nt(kv[i, 0, block + part], queries)
                scores = raw * (score_scale * math.log2(math.e)) + bias[block, part]
                s_buf[part] = scores
                row_max = jnp.maximum(row_max, jnp.max(scores, axis=0, keepdims=True))
            row_sum = jnp.zeros((1, tok), F32)
            delta = jnp.zeros((1, tok), F32)
            mixed = jnp.zeros((head_size, tok), F32)
            for part in range(3):
                weights = jnp.exp2(s_buf[part] - row_max)
                row_sum = row_sum + jnp.sum(weights, axis=0, keepdims=True)
                values = kv[i, 1, block + part]
                prob_grad = dot_nt(values, out_grad)
                delta = delta + jnp.sum(weights * prob_grad, axis=0, keepdims=True)
                s_buf[part] = weights
                dp_buf[part] = prob_grad
                mixed = mixed + dot_tn(values, weights.astype(BF16))
            inverse = 1.0 / row_sum
            delta = delta * inverse
            od[i, block, 0] = (mixed * inverse).T.astype(BF16)
            query_grad = jnp.zeros((head_size, tok), F32)
            for part in range(3):
                probs = s_buf[part] * inverse
                score_grad = (probs * (dp_buf[part] - delta)).astype(BF16)
                value_part = dot_nn(probs.astype(BF16), out_grad)
                key_part = dot_nn(score_grad, queries) * score_scale
                query_grad = query_grad + dot_tn(kv[i, 0, block + part], score_grad)
                at = block + part
                if block == 1 and part < 2:
                    key_part = key_part + grads[i, at, 0]
                    value_part = value_part + grads[i, at, 1]
                grads[i, at, 0] = key_part
                grads[i, at, 1] = value_part
            od[i, block, 1] = (query_grad * score_scale).T.astype(BF16)

    def total(i, block):
        return (grads[i, 2 + block] + halo_back[i, block].astype(F32)).astype(BF16)

    def finish(i):
        @pl.when(has_next)
        def _():
            send_back(i, other).wait_recv()

        last[i] = total(i, other)
        send_last(i).start()

    def forward(i):
        land_kv(i, 0).wait_recv()
        land_kv(i, 1).wait_recv()

        @pl.when(has_next)
        def _():
            send_fwd(i).start()

    def step(i, carry):
        land_qd(i).wait_recv()

        @pl.when(i + 2 < half)
        def _():
            send_kv(i + 2, 0).start()
            send_kv(i + 2, 1).start()

        @pl.when(i + 1 < half)
        def _():
            forward(i + 1)

        @pl.when(i + 2 < half)
        def _():
            send_qd(i + 2).start()

            @pl.when(has_next)
            def _():
                send_own(i + 2).start()

        @pl.when(has_prev)
        def _():
            land_own(i).wait_recv()
            land_fwd(i).wait_recv()

        @pl.when(i == half - 2)
        def _():
            send_od(0).start()

        compute(i)

        @pl.when(has_prev)
        def _():
            halo_out[i] = grads[i, 0:2].astype(BF16)
            send_back(i, other).start()
            send_back(i, x).start()

        @pl.when(i == half - 2)
        def _():
            for done in range(1, half - 1):
                send_od(done).start()
            for done in range(half - 2):
                finish(done)

        @pl.when(i == half - 1)
        def _():
            send_od(half - 1).start()
            finish(half - 2)

        for which in range(2):
            unpack(which, x * half + i, od[i, x, which])
        return carry

    forward(0)
    lax.fori_loop(0, half, step, 0)
    finish(half - 1)

    for i in range(half):
        @pl.when(has_next)
        def _():
            send_back(i, x).wait_recv()

        done = total(i, x)
        for which in range(2):
            unpack(2 + which, x * half + i, done[which])
        send_od(i).wait_recv()
        for which in range(2):
            unpack(which, other * half + i, od_in[i, which])
        if i == half - 1:
            write(0)
            write(1)
        send_last(i).wait_recv()
        for which in range(2):
            unpack(2 + which, other * half + i, last_in[i, which])
    write(2)
    write(3)

    send_spans().wait_send()
    for i in range(half):
        send_kv(i, 0).wait_send()
        send_kv(i, 1).wait_send()
        send_qd(i).wait_send()
        send_od(i).wait_send()
        send_last(i).wait_send()

    @pl.when(has_next)
    def _():
        for i in range(half):
            send_own(i).wait_send()
            send_fwd(i).wait_send()

    @pl.when(has_prev)
    def _():
        for i in range(half):
            send_back(i, other).wait_send()
            send_back(i, x).wait_send()


def per_device(count, queries, keys, values, out_grad, spans):
    tok, heads, head_size = queries.shape
    half = heads // 2
    flat = [a.reshape(tok * heads, head_size) for a in (keys, values, queries, out_grad)]
    vmem = pltpu.VMEM
    dma = pltpu.SemaphoreType.DMA
    blocks = 3 * 2 * heads // 2
    out = pl.pallas_call(
        functools.partial(kernel, count, tok, half, head_size),
        out_shape=vmem((4, tok * heads, head_size), BF16),
        in_specs=[pl.BlockSpec(memory_space=pltpu.HBM)] * 5,
        out_specs=pl.BlockSpec(memory_space=vmem),
        scratch_shapes=[
            vmem((4, heads * tok, head_size), BF16),
            vmem(spans.shape, jnp.int32),
            vmem((heads, 4, tok, head_size), BF16),
            vmem((4 * heads * tok, head_size), F32),
            vmem((half, 2, tok, head_size), BF16),
            vmem((half, 2, tok, head_size), BF16),
            vmem((half, 2, 4, tok, head_size), BF16),
            vmem((half, 2, 2, tok, head_size), BF16),
            vmem((8, tok), jnp.int32),
            vmem((8, tok), jnp.int32),
            vmem((2, 3, tok, tok), F32),
            vmem((3, tok, tok), F32),
            vmem((3, tok, tok), F32),
            vmem((half, 4, 2, tok, head_size), F32),
            vmem((half, 2, 2, tok, head_size), BF16),
            vmem((half, 2, 2, tok, head_size), BF16),
            vmem((half, 2, 2, tok, head_size), BF16),
            vmem((half, 2, tok, head_size), BF16),
            dma((4, PIECES)),
            dma,
            dma((2,)),
            dma((2, half, 2)),
            dma((2, half)),
            dma((2, half)),
            dma((2, half)),
            dma((2, half, 2)),
            dma((2, half)),
            dma((2, half)),
        ],
        compiler_params=pltpu.CompilerParams(
            collective_id=0, has_side_effects=True, vmem_limit_bytes=48 * 1024 * 1024
        ),
        cost_estimate=pl.CostEstimate(
            flops=blocks * 12 * tok * tok * head_size,
            bytes_accessed=8 * heads * tok * head_size,
            transcendentals=blocks * tok * tok,
        ),
    )(*[pltpu.with_memory_space_constraint(a, pltpu.HBM) for a in (*flat, spans)])
    return tuple(out[r].reshape(tok, heads, head_size) for r in range(4))


def solution(mesh):
    spec = P(("groups", "seq"), "heads", None)
    return jax.shard_map(
        functools.partial(per_device, mesh.shape["seq"]),
        mesh=mesh,
        in_specs=(spec,) * 4 + (P(None, ("groups", "seq")),),
        out_specs=(spec,) * 4,
        check_vma=False,
    )
```

```python
import functools
import math

import jax
import jax.numpy as jnp
from jax import lax
from jax.experimental import pallas as pl
from jax.experimental.pallas import tpu as pltpu
from jax.sharding import PartitionSpec as P

NEG = -1e30
PIECES = 2
MESH = pl.DeviceIdType.MESH
F32 = jnp.float32
BF16 = jnp.bfloat16


def dot_nt(a, b):
    return lax.dot_general(a, b, (((1,), (1,)), ((), ())), preferred_element_type=F32)


def dot_tn(a, b):
    return lax.dot_general(a, b, (((0,), (0,)), ((), ())), preferred_element_type=F32)


def dot_nn(a, b):
    return lax.dot_general(a, b, (((1,), (0,)), ((), ())), preferred_element_type=F32)


def kernel(
    count, tok, half, head_size,
    key_ref, value_ref, query_ref, grad_ref, spans_ref,
    out_ref,
    flat, spans_in, arg_ref, stage, od_in, last_in, kv, qd, span_own, span_other, bias, s_buf, dp_buf, grads, halo_out, halo_back, od, last,
    load_sem, span_load_sem, span_sem, kv_sem, qd_sem, own_sem, fwd_sem, back_sem, od_sem, last_sem,
):
    me = lax.axis_index("seq")
    x = lax.rem(me, 2)
    other = 1 - x
    pair = lax.div(me, 2)
    partner = me + 1 - 2 * x
    has_next = me + 2 < count
    has_prev = me >= 2
    score_scale = 1.0 / math.sqrt(head_size)

    def remote(src, dst, sems, at, to):
        return pltpu.make_async_remote_copy(
            src_ref=src,
            dst_ref=dst,
            send_sem=sems.at[(0,) + at],
            recv_sem=sems.at[(1,) + at],
            device_id={"seq": to},
            device_id_type=MESH,
        )

    def send_spans():
        return remote(span_own, span_other, span_sem, (), partner)

    def send_kv(i, which):
        src = arg_ref.at[other * half + i, which]
        return remote(src, kv.at[i, which, 2 + x], kv_sem, (i, which), partner)

    def send_qd(i):
        src = arg_ref.at[other * half + i, pl.ds(2, 2)]
        return remote(src, qd.at[i, x], qd_sem, (i,), partner)

    def send_own(i):
        src = arg_ref.at[x * half + i, pl.ds(0, 2)]
        return remote(src, kv.at[i, :, x], own_sem, (i,), me + 2)

    def send_fwd(i):
        return remote(kv.at[i, :, 2 + other], kv.at[i, :, other], fwd_sem, (i,), me + 2)

    def send_back(i, block):
        return remote(halo_out.at[i, block], halo_back.at[i, block], back_sem, (i, block), me - 2)

    def send_od(i):
        return remote(od.at[i, other], od_in.at[i], od_sem, (i,), partner)

    def send_last(i):
        return remote(last.at[i], last_in.at[i], last_sem, (i,), partner)

    def land_kv(i, which):
        dst = kv.at[i, which, 2 + other]
        return remote(arg_ref.at[0, which], dst, kv_sem, (i, which), partner)

    def land_qd(i):
        return remote(arg_ref.at[0, pl.ds(2, 2)], qd.at[i, other], qd_sem, (i,), partner)

    def land_own(i):
        return remote(arg_ref.at[0, pl.ds(0, 2)], kv.at[i, :, x], own_sem, (i,), partner)

    def land_fwd(i):
        return remote(arg_ref.at[0, pl.ds(0, 2)], kv.at[i, :, other], fwd_sem, (i,), partner)

    rows = 2 * half * tok

    def head_rows(which, head):
        return pl.ds(which * rows + head, tok, stride=2 * half)

    def pack(which, piece):
        span, part = rows // PIECES, tok // PIECES
        low = which * rows + piece * span
        stage[low : low + span, :] = flat[which, piece * span : (piece + 1) * span].astype(F32)
        for head in range(2 * half):
            block = stage[pl.ds(low + head, part, stride=2 * half), :]
            arg_ref[head, which, piece * part : (piece + 1) * part] = block.astype(BF16)

    def unpack(which, head, block):
        stage[head_rows(which, head), :] = block.astype(F32)

    def write(which):
        out_ref[which] = stage[which * rows : (which + 1) * rows, :].astype(BF16)

    inputs = (key_ref, value_ref, query_ref, grad_ref)

    def load(which, piece):
        at = pl.ds(piece * (rows // PIECES), rows // PIECES)
        return pltpu.make_async_copy(
            inputs[which].at[at], flat.at[which, at], load_sem.at[which, piece]
        )

    load_spans = pltpu.make_async_copy(spans_ref, spans_in, span_load_sem)
    for piece in range(PIECES):
        load(0, piece).start()
    for piece in range(PIECES):
        load(1, piece).start()
    load_spans.start()

    barrier = pltpu.get_barrier_semaphore()
    pl.semaphore_signal(barrier, inc=1, device_id={"seq": partner}, device_id_type=MESH)

    @pl.when(has_next)
    def _():
        pl.semaphore_signal(barrier, inc=1, device_id={"seq": me + 2}, device_id_type=MESH)

    @pl.when(has_prev)
    def _():
        pl.semaphore_signal(barrier, inc=1, device_id={"seq": me - 2}, device_id_type=MESH)

    for piece in range(PIECES):
        load(0, piece).wait()
        pack(0, piece)
    pl.semaphore_wait(barrier, 1 + has_next.astype(jnp.int32) + has_prev.astype(jnp.int32))
    send_kv(0, 0).start()
    send_kv(1, 0).start()

    for which in (2, 3):
        for piece in range(PIECES):
            load(which, piece).start()
    for piece in range(PIECES):
        load(1, piece).wait()
        pack(1, piece)
    send_kv(0, 1).start()
    send_kv(1, 1).start()

    @pl.when(has_next)
    def _():
        send_own(0).start()
        send_own(1).start()

    load_spans.wait()
    span_own[...] = jnp.zeros_like(span_own)
    span_own[0:3, :] = spans_in[...]
    send_spans().start()
    for piece in range(PIECES):
        load(2, piece).wait()
        pack(2, piece)
    for piece in range(PIECES):
        load(3, piece).wait()
        pack(3, piece)
    send_qd(0).start()
    send_qd(1).start()

    @pl.when(jnp.logical_not(has_prev))
    def _():
        for i in range(half):
            for which in range(2):
                kv[i, which, 0:2] = jnp.zeros((2, tok, head_size), BF16)

    @pl.when(jnp.logical_not(has_next))
    def _():
        halo_back[...] = jnp.zeros_like(halo_back)

    for i in range(half):
        kv[i, :, 2 + x] = arg_ref[x * half + i, 0:2]
        qd[i, x] = arg_ref[x * half + i, 2:4]

    send_spans().wait_recv()
    lane = lax.broadcasted_iota(jnp.int32, (1, tok), 1)
    for block in range(2):
        mine = x == block
        start_at = pair * (2 * tok) + block * tok
        low, chosen, rejected = [
            jnp.where(mine, span_own[r : r + 1, :], span_other[r : r + 1, :]) - start_at
            for r in range(3)
        ]
        chosen = jnp.where(lane >= rejected, chosen, 2 * tok)
        for part in range(3):
            at = lax.broadcasted_iota(jnp.int32, (tok, tok), 0) + (part - 2) * tok
            seen = (at >= low) & (at <= lane) & ((at < chosen) | (at >= rejected))
            bias[block, part] = jnp.where(seen, 0.0, NEG)

    def compute(i):
        for block in range(2):
            queries = qd[i, block, 0]
            out_grad = qd[i, block, 1]
            row_max = jnp.full((1, tok), -jnp.inf, F32)
            for part in range(3):
                raw = dot_nt(kv[i, 0, block + part], queries)
                scores = raw * (score_scale * math.log2(math.e)) + bias[block, part]
                s_buf[part] = scores
                row_max = jnp.maximum(row_max, jnp.max(scores, axis=0, keepdims=True))
            row_sum = jnp.zeros((1, tok), F32)
            delta = jnp.zeros((1, tok), F32)
            mixed = jnp.zeros((head_size, tok), F32)
            for part in range(3):
                weights = jnp.exp2(s_buf[part] - row_max)
                row_sum = row_sum + jnp.sum(weights, axis=0, keepdims=True)
                values = kv[i, 1, block + part]
                prob_grad = dot_nt(values, out_grad)
                delta = delta + jnp.sum(weights * prob_grad, axis=0, keepdims=True)
                s_buf[part] = weights
                dp_buf[part] = prob_grad
                mixed = mixed + dot_tn(values, weights.astype(BF16))
            inverse = 1.0 / row_sum
            delta = delta * inverse
            od[i, block, 0] = (mixed * inverse).T.astype(BF16)
            query_grad = jnp.zeros((head_size, tok), F32)
            for part in range(3):
                probs = s_buf[part] * inverse
                score_grad = (probs * (dp_buf[part] - delta)).astype(BF16)
                value_part = dot_nn(probs.astype(BF16), out_grad)
                key_part = dot_nn(score_grad, queries) * score_scale
                query_grad = query_grad + dot_tn(kv[i, 0, block + part], score_grad)
                at = block + part
                if block == 1 and part < 2:
                    key_part = key_part + grads[i, at, 0]
                    value_part = value_part + grads[i, at, 1]
                grads[i, at, 0] = key_part
                grads[i, at, 1] = value_part
            od[i, block, 1] = (query_grad * score_scale).T.astype(BF16)

    def total(i, block):
        return (grads[i, 2 + block] + halo_back[i, block].astype(F32)).astype(BF16)

    def finish(i):
        @pl.when(has_next)
        def _():
            send_back(i, other).wait_recv()

        last[i] = total(i, other)
        send_last(i).start()

    def forward(i):
        land_kv(i, 0).wait_recv()
        land_kv(i, 1).wait_recv()

        @pl.when(has_next)
        def _():
            send_fwd(i).start()

    def step(i, carry):
        land_qd(i).wait_recv()

        @pl.when(i + 2 < half)
        def _():
            send_kv(i + 2, 0).start()
            send_kv(i + 2, 1).start()

        @pl.when(i + 1 < half)
        def _():
            forward(i + 1)

        @pl.when(i + 2 < half)
        def _():
            send_qd(i + 2).start()

            @pl.when(has_next)
            def _():
                send_own(i + 2).start()

        @pl.when(has_prev)
        def _():
            land_own(i).wait_recv()
            land_fwd(i).wait_recv()

        compute(i)

        @pl.when(has_prev)
        def _():
            halo_out[i] = grads[i, 0:2].astype(BF16)
            send_back(i, other).start()
            send_back(i, x).start()

        send_od(i).start()

        @pl.when(i > 0)
        def _():
            finish(i - 1)

        for which in range(2):
            unpack(which, x * half + i, od[i, x, which])
        return carry

    forward(0)
    lax.fori_loop(0, half, step, 0)
    finish(half - 1)

    for i in range(half):
        @pl.when(has_next)
        def _():
            send_back(i, x).wait_recv()

        done = total(i, x)
        for which in range(2):
            unpack(2 + which, x * half + i, done[which])
        send_od(i).wait_recv()
        for which in range(2):
            unpack(which, other * half + i, od_in[i, which])
        if i == half - 1:
            write(0)
            write(1)
        send_last(i).wait_recv()
        for which in range(2):
            unpack(2 + which, other * half + i, last_in[i, which])
    write(2)
    write(3)

    send_spans().wait_send()
    for i in range(half):
        send_kv(i, 0).wait_send()
        send_kv(i, 1).wait_send()
        send_qd(i).wait_send()
        send_od(i).wait_send()
        send_last(i).wait_send()

    @pl.when(has_next)
    def _():
        for i in range(half):
            send_own(i).wait_send()
            send_fwd(i).wait_send()

    @pl.when(has_prev)
    def _():
        for i in range(half):
            send_back(i, other).wait_send()
            send_back(i, x).wait_send()


def per_device(count, queries, keys, values, out_grad, spans):
    tok, heads, head_size = queries.shape
    half = heads // 2
    flat = [a.reshape(tok * heads, head_size) for a in (keys, values, queries, out_grad)]
    vmem = pltpu.VMEM
    dma = pltpu.SemaphoreType.DMA
    blocks = 3 * 2 * heads // 2
    out = pl.pallas_call(
        functools.partial(kernel, count, tok, half, head_size),
        out_shape=vmem((4, tok * heads, head_size), BF16),
        in_specs=[pl.BlockSpec(memory_space=pltpu.HBM)] * 5,
        out_specs=pl.BlockSpec(memory_space=vmem),
        scratch_shapes=[
            vmem((4, heads * tok, head_size), BF16),
            vmem(spans.shape, jnp.int32),
            vmem((heads, 4, tok, head_size), BF16),
            vmem((4 * heads * tok, head_size), F32),
            vmem((half, 2, tok, head_size), BF16),
            vmem((half, 2, tok, head_size), BF16),
            vmem((half, 2, 4, tok, head_size), BF16),
            vmem((half, 2, 2, tok, head_size), BF16),
            vmem((8, tok), jnp.int32),
            vmem((8, tok), jnp.int32),
            vmem((2, 3, tok, tok), F32),
            vmem((3, tok, tok), F32),
            vmem((3, tok, tok), F32),
            vmem((half, 4, 2, tok, head_size), F32),
            vmem((half, 2, 2, tok, head_size), BF16),
            vmem((half, 2, 2, tok, head_size), BF16),
            vmem((half, 2, 2, tok, head_size), BF16),
            vmem((half, 2, tok, head_size), BF16),
            dma((4, PIECES)),
            dma,
            dma((2,)),
            dma((2, half, 2)),
            dma((2, half)),
            dma((2, half)),
            dma((2, half)),
            dma((2, half, 2)),
            dma((2, half)),
            dma((2, half)),
        ],
        compiler_params=pltpu.CompilerParams(
            collective_id=0, has_side_effects=True, vmem_limit_bytes=48 * 1024 * 1024
        ),
        cost_estimate=pl.CostEstimate(
            flops=blocks * 12 * tok * tok * head_size,
            bytes_accessed=8 * heads * tok * head_size,
            transcendentals=blocks * tok * tok,
        ),
    )(*[pltpu.with_memory_space_constraint(a, pltpu.HBM) for a in (*flat, spans)])
    return tuple(out[r].reshape(tok, heads, head_size) for r in range(4))


def solution(mesh):
    spec = P(("groups", "seq"), "heads", None)
    return jax.shard_map(
        functools.partial(per_device, mesh.shape["seq"]),
        mesh=mesh,
        in_specs=(spec,) * 4 + (P(None, ("groups", "seq")),),
        out_specs=(spec,) * 4,
        check_vma=False,
    )
```

```python
import functools
import math

import jax
import jax.numpy as jnp
from jax import lax
from jax.experimental import pallas as pl
from jax.experimental.pallas import tpu as pltpu
from jax.sharding import PartitionSpec as P

NEG = -1e30
PIECES = 4
MESH = pl.DeviceIdType.MESH
F32 = jnp.float32
BF16 = jnp.bfloat16


def dot_nt(a, b):
    return lax.dot_general(a, b, (((1,), (1,)), ((), ())), preferred_element_type=F32)


def dot_tn(a, b):
    return lax.dot_general(a, b, (((0,), (0,)), ((), ())), preferred_element_type=F32)


def dot_nn(a, b):
    return lax.dot_general(a, b, (((1,), (0,)), ((), ())), preferred_element_type=F32)


def kernel(
    count, tok, half, head_size,
    key_ref, value_ref, query_ref, grad_ref, spans_ref,
    out_ref,
    flat, spans_in, arg_ref, stage, od_in, last_in, kv, qd, span_own, span_other, bias, s_buf, dp_buf, grads, halo_out, halo_back, od, last,
    load_sem, span_load_sem, span_sem, kv_sem, qd_sem, own_sem, fwd_sem, back_sem, od_sem, last_sem,
):
    me = lax.axis_index("seq")
    x = lax.rem(me, 2)
    other = 1 - x
    pair = lax.div(me, 2)
    partner = me + 1 - 2 * x
    has_next = me + 2 < count
    has_prev = me >= 2
    score_scale = 1.0 / math.sqrt(head_size)

    def remote(src, dst, sems, at, to):
        return pltpu.make_async_remote_copy(
            src_ref=src,
            dst_ref=dst,
            send_sem=sems.at[(0,) + at],
            recv_sem=sems.at[(1,) + at],
            device_id={"seq": to},
            device_id_type=MESH,
        )

    def send_spans():
        return remote(span_own, span_other, span_sem, (), partner)

    def send_kv(i, which):
        src = arg_ref.at[other * half + i, which]
        return remote(src, kv.at[i, which, 2 + x], kv_sem, (i, which), partner)

    def send_qd(i):
        src = arg_ref.at[other * half + i, pl.ds(2, 2)]
        return remote(src, qd.at[i, x], qd_sem, (i,), partner)

    def send_own(i):
        src = arg_ref.at[x * half + i, pl.ds(0, 2)]
        return remote(src, kv.at[i, :, x], own_sem, (i,), me + 2)

    def send_fwd(i):
        return remote(kv.at[i, :, 2 + other], kv.at[i, :, other], fwd_sem, (i,), me + 2)

    def send_back(i, block):
        return remote(halo_out.at[i, block], halo_back.at[i, block], back_sem, (i, block), me - 2)

    def send_od(i):
        return remote(od.at[i, other], od_in.at[i], od_sem, (i,), partner)

    def send_last(i):
        return remote(last.at[i], last_in.at[i], last_sem, (i,), partner)

    def land_kv(i, which):
        dst = kv.at[i, which, 2 + other]
        return remote(arg_ref.at[0, which], dst, kv_sem, (i, which), partner)

    def land_qd(i):
        return remote(arg_ref.at[0, pl.ds(2, 2)], qd.at[i, other], qd_sem, (i,), partner)

    def land_own(i):
        return remote(arg_ref.at[0, pl.ds(0, 2)], kv.at[i, :, x], own_sem, (i,), partner)

    def land_fwd(i):
        return remote(arg_ref.at[0, pl.ds(0, 2)], kv.at[i, :, other], fwd_sem, (i,), partner)

    rows = 2 * half * tok

    def head_rows(which, head):
        return pl.ds(which * rows + head, tok, stride=2 * half)

    def pack(which, piece):
        span, part = rows // PIECES, tok // PIECES
        low = which * rows + piece * span
        stage[low : low + span, :] = flat[which, piece * span : (piece + 1) * span].astype(F32)
        for head in range(2 * half):
            block = stage[pl.ds(low + head, part, stride=2 * half), :]
            arg_ref[head, which, piece * part : (piece + 1) * part] = block.astype(BF16)

    def unpack(which, head, block):
        stage[head_rows(which, head), :] = block.astype(F32)

    def write(which):
        out_ref[which] = stage[which * rows : (which + 1) * rows, :].astype(BF16)

    inputs = (key_ref, value_ref, query_ref, grad_ref)

    def load(which, piece):
        at = pl.ds(piece * (rows // PIECES), rows // PIECES)
        return pltpu.make_async_copy(
            inputs[which].at[at], flat.at[which, at], load_sem.at[which, piece]
        )

    load_spans = pltpu.make_async_copy(spans_ref, spans_in, span_load_sem)
    for piece in range(PIECES):
        load(0, piece).start()
    for piece in range(PIECES):
        load(1, piece).start()
    load_spans.start()

    barrier = pltpu.get_barrier_semaphore()
    pl.semaphore_signal(barrier, inc=1, device_id={"seq": partner}, device_id_type=MESH)

    @pl.when(has_next)
    def _():
        pl.semaphore_signal(barrier, inc=1, device_id={"seq": me + 2}, device_id_type=MESH)

    @pl.when(has_prev)
    def _():
        pl.semaphore_signal(barrier, inc=1, device_id={"seq": me - 2}, device_id_type=MESH)

    for piece in range(PIECES):
        load(0, piece).wait()
        pack(0, piece)
    pl.semaphore_wait(barrier, 1 + has_next.astype(jnp.int32) + has_prev.astype(jnp.int32))
    send_kv(0, 0).start()
    send_kv(1, 0).start()

    for which in (2, 3):
        for piece in range(PIECES):
            load(which, piece).start()
    for piece in range(PIECES):
        load(1, piece).wait()
        pack(1, piece)
    send_kv(0, 1).start()
    send_kv(1, 1).start()

    @pl.when(has_next)
    def _():
        send_own(0).start()
        send_own(1).start()

    load_spans.wait()
    span_own[...] = jnp.zeros_like(span_own)
    span_own[0:3, :] = spans_in[...]
    send_spans().start()
    for piece in range(PIECES):
        load(2, piece).wait()
        pack(2, piece)
    for piece in range(PIECES):
        load(3, piece).wait()
        pack(3, piece)
    send_qd(0).start()
    send_qd(1).start()

    @pl.when(jnp.logical_not(has_prev))
    def _():
        for i in range(half):
            for which in range(2):
                kv[i, which, 0:2] = jnp.zeros((2, tok, head_size), BF16)

    @pl.when(jnp.logical_not(has_next))
    def _():
        halo_back[...] = jnp.zeros_like(halo_back)

    for i in range(half):
        kv[i, :, 2 + x] = arg_ref[x * half + i, 0:2]
        qd[i, x] = arg_ref[x * half + i, 2:4]

    send_spans().wait_recv()
    lane = lax.broadcasted_iota(jnp.int32, (1, tok), 1)
    for block in range(2):
        mine = x == block
        start_at = pair * (2 * tok) + block * tok
        low, chosen, rejected = [
            jnp.where(mine, span_own[r : r + 1, :], span_other[r : r + 1, :]) - start_at
            for r in range(3)
        ]
        chosen = jnp.where(lane >= rejected, chosen, 2 * tok)
        for part in range(3):
            at = lax.broadcasted_iota(jnp.int32, (tok, tok), 0) + (part - 2) * tok
            seen = (at >= low) & (at <= lane) & ((at < chosen) | (at >= rejected))
            bias[block, part] = jnp.where(seen, 0.0, NEG)

    def compute(i):
        for block in range(2):
            queries = qd[i, block, 0]
            out_grad = qd[i, block, 1]
            row_max = jnp.full((1, tok), -jnp.inf, F32)
            for part in range(3):
                raw = dot_nt(kv[i, 0, block + part], queries)
                scores = raw * (score_scale * math.log2(math.e)) + bias[block, part]
                s_buf[part] = scores
                row_max = jnp.maximum(row_max, jnp.max(scores, axis=0, keepdims=True))
            row_sum = jnp.zeros((1, tok), F32)
            delta = jnp.zeros((1, tok), F32)
            mixed = jnp.zeros((head_size, tok), F32)
            for part in range(3):
                weights = jnp.exp2(s_buf[part] - row_max)
                row_sum = row_sum + jnp.sum(weights, axis=0, keepdims=True)
                values = kv[i, 1, block + part]
                prob_grad = dot_nt(values, out_grad)
                delta = delta + jnp.sum(weights * prob_grad, axis=0, keepdims=True)
                s_buf[part] = weights
                dp_buf[part] = prob_grad
                mixed = mixed + dot_tn(values, weights.astype(BF16))
            inverse = 1.0 / row_sum
            delta = delta * inverse
            od[i, block, 0] = (mixed * inverse).T.astype(BF16)
            query_grad = jnp.zeros((head_size, tok), F32)
            for part in range(3):
                probs = s_buf[part] * inverse
                score_grad = (probs * (dp_buf[part] - delta)).astype(BF16)
                value_part = dot_nn(probs.astype(BF16), out_grad)
                key_part = dot_nn(score_grad, queries) * score_scale
                query_grad = query_grad + dot_tn(kv[i, 0, block + part], score_grad)
                at = block + part
                if block == 1 and part < 2:
                    key_part = key_part + grads[i, at, 0]
                    value_part = value_part + grads[i, at, 1]
                grads[i, at, 0] = key_part
                grads[i, at, 1] = value_part
            od[i, block, 1] = (query_grad * score_scale).T.astype(BF16)

    def total(i, block):
        return (grads[i, 2 + block] + halo_back[i, block].astype(F32)).astype(BF16)

    def finish(i):
        @pl.when(has_next)
        def _():
            send_back(i, other).wait_recv()

        last[i] = total(i, other)
        send_last(i).start()

    def forward(i):
        land_kv(i, 0).wait_recv()
        land_kv(i, 1).wait_recv()

        @pl.when(has_next)
        def _():
            send_fwd(i).start()

    def step(i, carry):
        land_qd(i).wait_recv()

        @pl.when(i + 2 < half)
        def _():
            send_kv(i + 2, 0).start()
            send_kv(i + 2, 1).start()

        @pl.when(i + 1 < half)
        def _():
            forward(i + 1)

        @pl.when(i + 2 < half)
        def _():
            send_qd(i + 2).start()

            @pl.when(has_next)
            def _():
                send_own(i + 2).start()

        @pl.when(has_prev)
        def _():
            land_own(i).wait_recv()
            land_fwd(i).wait_recv()

        @pl.when(i == half - 2)
        def _():
            send_od(0).start()

        compute(i)

        @pl.when(has_prev)
        def _():
            halo_out[i] = grads[i, 0:2].astype(BF16)
            send_back(i, other).start()
            send_back(i, x).start()

        @pl.when(i == half - 2)
        def _():
            for done in range(1, half - 1):
                send_od(done).start()
            for done in range(half - 2):
                finish(done)

        @pl.when(i == half - 1)
        def _():
            send_od(half - 1).start()
            finish(half - 2)

        for which in range(2):
            unpack(which, x * half + i, od[i, x, which])
        return carry

    forward(0)
    lax.fori_loop(0, half, step, 0)
    finish(half - 1)

    for i in range(half):
        @pl.when(has_next)
        def _():
            send_back(i, x).wait_recv()

        done = total(i, x)
        for which in range(2):
            unpack(2 + which, x * half + i, done[which])
        send_od(i).wait_recv()
        for which in range(2):
            unpack(which, other * half + i, od_in[i, which])
        if i == half - 1:
            write(0)
            write(1)
        send_last(i).wait_recv()
        for which in range(2):
            unpack(2 + which, other * half + i, last_in[i, which])
    write(2)
    write(3)

    send_spans().wait_send()
    for i in range(half):
        send_kv(i, 0).wait_send()
        send_kv(i, 1).wait_send()
        send_qd(i).wait_send()
        send_od(i).wait_send()
        send_last(i).wait_send()

    @pl.when(has_next)
    def _():
        for i in range(half):
            send_own(i).wait_send()
            send_fwd(i).wait_send()

    @pl.when(has_prev)
    def _():
        for i in range(half):
            send_back(i, other).wait_send()
            send_back(i, x).wait_send()


def per_device(count, queries, keys, values, out_grad, spans):
    tok, heads, head_size = queries.shape
    half = heads // 2
    flat = [a.reshape(tok * heads, head_size) for a in (keys, values, queries, out_grad)]
    vmem = pltpu.VMEM
    dma = pltpu.SemaphoreType.DMA
    blocks = 3 * 2 * heads // 2
    out = pl.pallas_call(
        functools.partial(kernel, count, tok, half, head_size),
        out_shape=vmem((4, tok * heads, head_size), BF16),
        in_specs=[pl.BlockSpec(memory_space=pltpu.HBM)] * 5,
        out_specs=pl.BlockSpec(memory_space=vmem),
        scratch_shapes=[
            vmem((4, heads * tok, head_size), BF16),
            vmem(spans.shape, jnp.int32),
            vmem((heads, 4, tok, head_size), BF16),
            vmem((4 * heads * tok, head_size), F32),
            vmem((half, 2, tok, head_size), BF16),
            vmem((half, 2, tok, head_size), BF16),
            vmem((half, 2, 4, tok, head_size), BF16),
            vmem((half, 2, 2, tok, head_size), BF16),
            vmem((8, tok), jnp.int32),
            vmem((8, tok), jnp.int32),
            vmem((2, 3, tok, tok), F32),
            vmem((3, tok, tok), F32),
            vmem((3, tok, tok), F32),
            vmem((half, 4, 2, tok, head_size), F32),
            vmem((half, 2, 2, tok, head_size), BF16),
            vmem((half, 2, 2, tok, head_size), BF16),
            vmem((half, 2, 2, tok, head_size), BF16),
            vmem((half, 2, tok, head_size), BF16),
            dma((4, PIECES)),
            dma,
            dma((2,)),
            dma((2, half, 2)),
            dma((2, half)),
            dma((2, half)),
            dma((2, half)),
            dma((2, half, 2)),
            dma((2, half)),
            dma((2, half)),
        ],
        compiler_params=pltpu.CompilerParams(
            collective_id=0, has_side_effects=True, vmem_limit_bytes=48 * 1024 * 1024
        ),
        cost_estimate=pl.CostEstimate(
            flops=blocks * 12 * tok * tok * head_size,
            bytes_accessed=8 * heads * tok * head_size,
            transcendentals=blocks * tok * tok,
        ),
    )(*[pltpu.with_memory_space_constraint(a, pltpu.HBM) for a in (*flat, spans)])
    return tuple(out[r].reshape(tok, heads, head_size) for r in range(4))


def solution(mesh):
    spec = P(("groups", "seq"), "heads", None)
    return jax.shard_map(
        functools.partial(per_device, mesh.shape["seq"]),
        mesh=mesh,
        in_specs=(spec,) * 4 + (P(None, ("groups", "seq")),),
        out_specs=(spec,) * 4,
        check_vma=False,
    )
```
